128 devices in a mesh: depth: 2 (over core), tile: 64 (over x, y, z).
Axes of the slice: x: 4, y: 4, z: 4, core: 2. Of those that a mesh axis runs over, the one named last changes fastest.
Arguments:
- specimen: float32 [4, 2, 8192, 2048], P('depth', None, 'tile'), may hold values from -4.2 to 4.2
- scan_offsets: int32 [128, 2], P('tile'), may hold values from 0 to 7936, as said below
- probe_wave: float32 [2, 256, 256], replicated, may hold values from -4.2 to 4.2
- fresnel_phase: float32 [256, 256], replicated, may hold values from -3.140625 to 3.140625
- measured: float32 [128, 256, 256], P('tile'), may hold values from 0 to 3
Outputs:
- specimen_gradient: float32 [4, 2, 8192, 2048], P('depth', None, 'tile')
The draws below stay inside these ranges and needn't reach their ends.
Inputs may be any that keep to these rules, and one draw needn't show every extreme that they name: `scan_offsets`: A position held by tile index d (positions d * 2 to (d + 1) * 2 - 1) has its top row between max(0, (d - 1) * 128) and min(d * 128, 7936), and its left column at most 1792.
All inputs are finite; a program needn't handle non-finite values.
Results may differ from the reference program's by a relative error of at most 0.0003.
Values sent between devices are 32-bit elements; how exact they have to be, the bound alone decides.
A program may use at most 128 MiB of HBM per device.

```python
import jax
import jax.numpy as jnp
from jax import lax

PSZ = 256
P_DEV = 2
OBJ_W = 2048
ROWS_DEV = 128
NROWS = 8192
SLICES = 4
POSITIONS = 128


def draw_scan_offsets(key, part):
    row_key = jax.random.fold_in(key, 11)
    col_key = jax.random.fold_in(key, 23)
    holder = jnp.arange(POSITIONS, dtype=jnp.int32) // P_DEV
    lowest = jnp.maximum(0, (holder - 1) * ROWS_DEV)
    highest = jnp.minimum(holder * ROWS_DEV, NROWS - PSZ)
    top_rows = jax.random.randint(row_key, (POSITIONS,), lowest, highest + 1)
    left_cols = jax.random.randint(col_key, (POSITIONS,), 0, OBJ_W - PSZ + 1)
    return jnp.stack([top_rows, left_cols], 1).astype(jnp.int32)


def block_scale(own_key, dims, split, smallest, top_value):
    gain = 1.0
    for dim, shards_of in split:
        heights = jax.random.uniform(jax.random.fold_in(jax.random.fold_in(own_key, 6), dim), (shards_of,), jnp.float32, smallest / len(split), top_value / len(split))
        gain = gain * jnp.repeat(jnp.exp(heights), dims[dim] // shards_of).reshape((-1,) + (1,) * (len(dims) - 1 - dim))
    return gain


def bell_draw(key, dims, scale, reach, shards=(), kind=jnp.bfloat16):
    level = block_scale(key, dims, shards, -0.22, 0.18) if shards else 1.0
    array = jax.random.normal(key, dims, jnp.float32) * scale * level
    return jnp.minimum(jnp.maximum(array, -reach), reach).astype(kind)


def setup_inputs(seed: int = 0) -> dict:
    key_of = jax.random.split(jax.random.key(seed), 6)
    specimen = bell_draw(key_of[0], (SLICES, 2, NROWS, OBJ_W), 0.7, 4.2, ((0, 2), (2, 64)), jnp.float32)
    scan_offsets = draw_scan_offsets(jax.random.fold_in(key_of[5], 71), 0)
    probe_wave = bell_draw(key_of[2], (2, PSZ, PSZ), 0.7, 4.2, (), jnp.float32)
    fresnel_phase = jnp.clip(jax.random.uniform(key_of[3], (PSZ, PSZ), jnp.float32, -3.140625, 3.140625), -3.140625, 3.140625)
    measured = jnp.clip(3.0 * jax.random.uniform(key_of[4], (POSITIONS, PSZ, PSZ), jnp.float32) ** block_scale(key_of[4], (POSITIONS, PSZ, PSZ), ((0, 64),), -0.2, 0.2), 0.0, 3.0)
    return dict(specimen=specimen, scan_offsets=scan_offsets, probe_wave=probe_wave, fresnel_phase=fresnel_phase, measured=measured)


def reference(specimen, scan_offsets, probe_wave, fresnel_phase, measured):
    layers = specimen.shape[0]
    complex_field = lax.complex(specimen[:, 0], specimen[:, 1])
    probe_complex = lax.complex(probe_wave[0], probe_wave[1])
    kernel = lax.complex(jnp.cos(fresnel_phase), jnp.sin(fresnel_phase))

    def forward(values):
        return jnp.fft.fft2(values, norm="ortho")

    def inverse(values):
        return jnp.fft.ifft2(values, norm="ortho")

    def one_position(gradient, inputs):
        offsets, target = inputs
        anchor = jnp.zeros((), jnp.int32)
        start = (anchor, offsets[0].astype(jnp.int32), offsets[1].astype(jnp.int32))
        patches = lax.dynamic_slice(complex_field, start, (layers, PSZ, PSZ))
        current = probe_complex
        wave_list = []
        passed = current
        for layer_index in range(layers):
            wave_list.append(current)
            passed = current * patches[layer_index]
            if layer_index + 1 < layers:
                current = inverse(kernel * forward(passed))
        spectrum = forward(passed)
        residue = 2.0 * (jnp.real(spectrum) ** 2 + jnp.imag(spectrum) ** 2 - target)
        current = inverse(residue * spectrum)
        grad_list = [None] * layers
        for layer_index in reversed(range(layers)):
            grad_list[layer_index] = jnp.conj(wave_list[layer_index]) * current
            if layer_index > 0:
                current = inverse(jnp.conj(kernel) * forward(jnp.conj(patches[layer_index]) * current))
        update = jnp.stack(grad_list, 0)
        region = lax.dynamic_slice(gradient, start, (layers, PSZ, PSZ))
        gradient = lax.dynamic_update_slice(gradient, region + update, start)
        return gradient, None

    gradient, unused = lax.scan(one_position, jnp.zeros_like(complex_field), (scan_offsets.astype(jnp.int32), measured))
    return jnp.stack([jnp.real(gradient), jnp.imag(gradient)], 1)
```

```python
import functools

import jax
import jax.numpy as jnp
import ml_dtypes
import numpy as np
from jax import lax
from jax.experimental import pallas as pl
from jax.experimental.pallas import tpu as pltpu
from jax.sharding import PartitionSpec as P

MESH = pl.DeviceIdType.MESH
F32 = jnp.float32
BF16 = jnp.bfloat16
HALF = 128
FULL = 256


def halves(matrix):
    high = matrix.astype(ml_dtypes.bfloat16)
    low = (matrix - high.astype(np.float64)).astype(ml_dtypes.bfloat16)
    return high, low


def dft_tables():
    n = np.arange(HALF)
    tables = []
    for parity in (0, 1):
        angle = 2.0 * np.pi * ((n[:, None] * (2 * n[None, :] + parity)) % FULL) / FULL
        cosine, sine = np.cos(angle) / 16.0, np.sin(angle) / 16.0
        right = np.block([[cosine, -sine], [sine, cosine]])
        tables.append(right)
    parts = [halves(m) for right in tables for m in (right, right.T)]
    return np.stack([np.stack(p) for p in parts])


def order_tables():
    order = np.concatenate([np.arange(0, FULL, 2), np.arange(1, FULL, 2)])
    right = np.zeros((FULL, FULL), np.float32)
    right[order, np.arange(FULL)] = 1.0
    return np.stack([right, right.T]).astype(ml_dtypes.bfloat16)


def dot(a, b):
    return jnp.dot(a, b, preferred_element_type=F32)


def two_parts(x):
    high = x.astype(BF16)
    low = (x - high.astype(F32)).astype(BF16)
    return high, low


def exact_right(x, ones):
    high = x.astype(BF16)
    rest = x - high.astype(F32)
    middle = rest.astype(BF16)
    low = (rest - middle.astype(F32)).astype(BF16)
    return (dot(high, ones) + dot(middle, ones)) + dot(low, ones)


def exact_left(ones, x):
    high = x.astype(BF16)
    rest = x - high.astype(F32)
    middle = rest.astype(BF16)
    low = (rest - middle.astype(F32)).astype(BF16)
    return (dot(ones, high) + dot(ones, middle)) + dot(ones, low)


def times_right(x, table):
    high, low = two_parts(x)
    return dot(high, table[0]) + (dot(low, table[0]) + dot(high, table[1]))


def times_left(table, x):
    high, low = two_parts(x)
    return dot(table[0], high) + (dot(table[0], low) + dot(table[1], high))


EVEN, EVEN_T, ODD, ODD_T = range(4)


def forward_transform(x_ref, z_ref, tab):
    re, im = x_ref[0], x_ref[1]
    even = jnp.concatenate([re[:, :HALF] + re[:, HALF:], im[:, :HALF] + im[:, HALF:]], 1)
    odd = jnp.concatenate([re[:, :HALF] - re[:, HALF:], im[:, :HALF] - im[:, HALF:]], 1)
    ye = times_right(even, tab.at[EVEN])
    yo = times_right(odd, tab.at[ODD])
    re = jnp.concatenate([ye[:, :HALF], yo[:, :HALF]], 1)
    im = jnp.concatenate([ye[:, HALF:], yo[:, HALF:]], 1)
    z_ref[0] = times_left(tab.at[EVEN_T], jnp.concatenate([re[:HALF] + re[HALF:], im[:HALF] + im[HALF:]], 0))
    z_ref[1] = times_left(tab.at[ODD_T], jnp.concatenate([re[:HALF] - re[HALF:], im[:HALF] - im[HALF:]], 0))


def inverse_transform(z_ref, out, tab):
    a = times_left(tab.at[EVEN], z_ref[0])
    b = times_left(tab.at[ODD], z_ref[1])
    total, rest = a + b, a - b
    re = jnp.concatenate([total[:HALF], rest[:HALF]], 0)
    im = jnp.concatenate([total[HALF:], rest[HALF:]], 0)
    a = times_right(jnp.concatenate([re[:, :HALF], im[:, :HALF]], 1), tab.at[EVEN_T])
    b = times_right(jnp.concatenate([re[:, HALF:], im[:, HALF:]], 1), tab.at[ODD_T])
    total, rest = a + b, a - b
    out[0] = jnp.concatenate([total[:, :HALF], rest[:, :HALF]], 1)
    out[1] = jnp.concatenate([total[:, HALF:], rest[:, HALF:]], 1)


def column_block(column, width):
    block = jnp.minimum(lax.shift_right_logical(column, 7), width // HALF - 3)
    return block, column - block * HALF


def take_window(spec, layer, component, column, width):
    block, shift = column_block(column, width)
    lane = lax.broadcasted_iota(jnp.int32, (HALF, HALF), 1)
    mixed = jnp.where(lane >= shift, spec[layer, component, block], spec[layer, component, block + 2])
    return mixed, spec[layer, component, block + 1]


def main_kernel(
    tiles, width,
    offs, spec_hbm, probe_hbm, phase_hbm, meas_hbm, tab_hbm, perm_hbm,
    grads, offs_out,
    spec, probe, phase, meas, tab, perm,
    staged, near, own_staged, own, patch, field, x_buf, z_buf, kern, update, offs_land,
    block_sem, load_sem, off_send, off_recv, in_send, in_recv, sib_send, sib_recv,
    out_send, out_recv, mid_send, mid_recv, mid_local,
):
    me = lax.axis_index("tile")
    core = lax.axis_index("depth")
    other = 1 - core
    has_above = me > 0
    has_below = me < tiles - 1
    above = jnp.maximum(me - 1, 0)
    below = jnp.minimum(me + 1, tiles - 1)

    barrier = pltpu.get_barrier_semaphore()
    pl.semaphore_signal(barrier, inc=1, device_id=(other, me), device_id_type=MESH)

    @pl.when(has_above)
    def _():
        for d in (0, 1):
            pl.semaphore_signal(barrier, inc=1, device_id=(d, above), device_id_type=MESH)

    @pl.when(has_below)
    def _():
        for d in (0, 1):
            pl.semaphore_signal(barrier, inc=1, device_id=(d, below), device_id_type=MESH)

    blocks = width // HALF

    def block_copy(b):
        return pltpu.make_async_copy(
            spec_hbm.at[:, :, :, pl.ds(b * HALF, HALF)], spec.at[:, :, b], block_sem.at[b]
        )

    loads = [
        pltpu.make_async_copy(tab_hbm, tab, load_sem.at[0]),
        pltpu.make_async_copy(perm_hbm, perm, load_sem.at[1]),
        pltpu.make_async_copy(probe_hbm, probe, load_sem.at[2]),
        pltpu.make_async_copy(phase_hbm, phase, load_sem.at[3]),
        pltpu.make_async_copy(meas_hbm.at[core], meas, load_sem.at[4]),
    ]
    for b in range(blocks):
        block_copy(b).start()
    for copy in loads:
        copy.start()
    pl.semaphore_wait(barrier, 1 + 2 * has_above.astype(jnp.int32) + 2 * has_below.astype(jnp.int32))

    def offsets_copy(side):
        return pltpu.make_async_remote_copy(
            src_ref=offs, dst_ref=offs_land.at[1 - side], send_sem=off_send.at[side], recv_sem=off_recv.at[1 - side],
            device_id=(core, above if side == 0 else below), device_id_type=MESH,
        )

    sides = ((0, has_above), (1, has_below))
    for side, there in sides:
        pl.when(there)(offsets_copy(side).start)

    for b in range(blocks):
        block_copy(b).wait()
    for layer in (0, 1):
        for c in (0, 1):
            mixed, pure = take_window(spec, layer, c, offs[other, 1], width)
            own_staged[layer, c, :, :HALF] = mixed
            own_staged[layer, c, :, HALF:] = pure

    def sibling_copy(layer):
        return pltpu.make_async_remote_copy(
            src_ref=own_staged.at[layer], dst_ref=own.at[2 * core + layer], send_sem=sib_send.at[layer],
            recv_sem=sib_recv.at[layer], device_id=(other, me), device_id_type=MESH,
        )

    for layer in (0, 1):
        sibling_copy(layer).start()
    for layer in (0, 1):
        for c in (0, 1):
            mixed, pure = take_window(spec, layer, c, offs[core, 1], width)
            own[2 * core + layer, c, :, :HALF] = mixed
            own[2 * core + layer, c, :, HALF:] = pure

    def window_copy(position, layer, side):
        return pltpu.make_async_remote_copy(
            src_ref=staged.at[side, position, layer], dst_ref=near.at[1 - side, 2 * core + layer],
            send_sem=in_send.at[side, position, layer], recv_sem=in_recv.at[1 - side, 2 * core + layer],
            device_id=(position, above if side == 0 else below), device_id_type=MESH,
        )

    for side, there in sides:
        @pl.when(there)
        def _(side=side):
            pltpu.make_async_remote_copy(
                src_ref=offs, dst_ref=offs_land.at[side], send_sem=off_send.at[side], recv_sem=off_recv.at[side],
                device_id=(core, above if side == 0 else below), device_id_type=MESH,
            ).wait_recv()

    for position in (0, 1):
        for layer in (0, 1):
            for side, there in sides:
                @pl.when(there)
                def _(position=position, layer=layer, side=side):
                    for c in (0, 1):
                        mixed, pure = take_window(spec, layer, c, offs_land[side, position, 1], width)
                        staged[side, position, layer, c, :, :HALF] = mixed
                        staged[side, position, layer, c, :, HALF:] = pure
                    window_copy(position, layer, side).start()

    for side, there in sides:
        for position in (0, 1):
            first = offs_land[side, position, 0] - (me - 2 + 2 * side) * HALF
            offs_out[side, position, 0] = jnp.where(there, first, HALF * side)
            offs_out[side, position, 1] = jnp.where(there, offs_land[side, position, 1], 0)

    first = offs[core, 0] - (me - 1) * HALF
    unused, shift = column_block(offs[core, 1], width)
    for copy in loads:
        copy.wait()
    phases = exact_right(exact_left(perm[1], phase[...]), perm[0])
    kern[0] = jnp.cos(phases)
    kern[1] = jnp.sin(phases)
    meas[...] = exact_right(exact_left(perm[1], meas[...]), perm[0])
    rows = lax.broadcasted_iota(jnp.int32, (FULL, FULL), 0)
    cols = lax.broadcasted_iota(jnp.int32, (FULL, FULL), 1)
    turn = jnp.where(((cols + first) & (FULL - 1)) == rows, 1.0, 0.0).astype(BF16)
    slide = jnp.where(((rows + shift) & (FULL - 1)) == cols, 1.0, 0.0).astype(BF16)
    for c in (0, 1):
        field[0, c] = exact_right(exact_left(turn, probe[c]), slide)

    for layer in (0, 1):
        pltpu.make_async_remote_copy(
            src_ref=own_staged.at[layer], dst_ref=own.at[2 * other + layer], send_sem=sib_send.at[layer],
            recv_sem=sib_recv.at[layer], device_id=(other, me), device_id_type=MESH,
        ).wait_recv()

    half_rows = lax.broadcasted_iota(jnp.int32, (HALF, FULL), 0)

    def update_copy(s, side):
        target = s // 2
        return pltpu.make_async_remote_copy(
            src_ref=update.at[s, :, pl.ds(0, HALF)], dst_ref=grads.at[s - 2 * target, 2 * (1 - side) + core],
            send_sem=out_send.at[side, s], recv_sem=out_recv.at[s - 2 * target, 2 * (1 - side) + core],
            device_id=(target, above if side == 0 else below), device_id_type=MESH,
        )

    def middle_copy(layer):
        return pltpu.make_async_remote_copy(
            src_ref=update.at[2 * other + layer, :, pl.ds(HALF, HALF)], dst_ref=grads.at[layer, 4 + core],
            send_sem=mid_send.at[layer], recv_sem=mid_recv.at[layer], device_id=(other, me), device_id_type=MESH,
        )

    def middle_local(layer):
        return pltpu.make_async_copy(
            update.at[2 * core + layer, :, pl.ds(HALF, HALF)], grads.at[layer, 4 + core], mid_local.at[layer]
        )

    def step(i, carry):
        @pl.when(i <= 3)
        def _():
            for side, there in sides:
                @pl.when(there)
                def _(side=side):
                    pltpu.make_async_remote_copy(
                        src_ref=staged.at[side, 0, 0], dst_ref=near.at[side, i], send_sem=in_send.at[side, 0, 0],
                        recv_sem=in_recv.at[side, i], device_id=(core, above if side == 0 else below),
                        device_id_type=MESH,
                    ).wait_recv()
            top = [jnp.where(half_rows >= first, near[0, i, c], near[1, i, c]) for c in (0, 1)]
            bottom = [own[i, c] for c in (0, 1)]
            for c in (0, 1):
                patch[i, c, :HALF] = top[c]
                patch[i, c, HALF:] = bottom[c]
            for part, (pr, pi) in enumerate((top, bottom)):
                span = pl.ds(part * HALF, HALF)
                wr, wi = field[i, 0, span], field[i, 1, span]
                x_buf[0, span] = wr * pr - wi * pi
                x_buf[1, span] = wr * pi + wi * pr

        @pl.when(i > 3)
        def _():
            pr, pi = patch[7 - i, 0], patch[7 - i, 1]
            ar, ai = field[i, 0], field[i, 1]
            x_buf[0] = pr * ar + pi * ai
            x_buf[1] = pr * ai - pi * ar

        forward_transform(x_buf, z_buf, tab)

        @pl.when(i == 3)
        def _():
            for parity in (0, 1):
                zr, zi = z_buf[parity, :HALF], z_buf[parity, HALF:]
                e = 2.0 * (zr * zr + zi * zi - meas[parity * HALF : (parity + 1) * HALF])
                z_buf[parity, :HALF] = e * zr
                z_buf[parity, HALF:] = e * zi

        @pl.when(i != 3)
        def _():
            sign = jnp.where(i < 3, 1.0, -1.0)
            for parity in (0, 1):
                span = slice(parity * HALF, (parity + 1) * HALF)
                zr, zi = z_buf[parity, :HALF], z_buf[parity, HALF:]
                kr, ki = kern[0, span], sign * kern[1, span]
                z_buf[parity, :HALF] = kr * zr - ki * zi
                z_buf[parity, HALF:] = kr * zi + ki * zr

        inverse_transform(z_buf, field.at[i + 1], tab)

        @pl.when(i >= 3)
        def _():
            s = 6 - i
            wr, wi = field[s, 0], field[s, 1]
            ar, ai = field[i + 1, 0], field[i + 1, 1]
            update[s, 0] = wr * ar + wi * ai
            update[s, 1] = wr * ai - wi * ar
            for side, there in sides:
                @pl.when(there)
                def _(side=side):
                    update_copy(s, side).start()
            for layer in (0, 1):
                pl.when(s == 2 * other + layer)(middle_copy(layer).start)
                pl.when(s == 2 * core + layer)(middle_local(layer).start)

        return carry

    lax.fori_loop(0, 7, step, 0)

    for layer in (0, 1):
        middle_local(layer).wait()
        middle_copy(layer).wait_send()
        pltpu.make_async_remote_copy(
            src_ref=update.at[0, :, pl.ds(HALF, HALF)], dst_ref=grads.at[layer, 4 + other],
            send_sem=mid_send.at[layer], recv_sem=mid_recv.at[layer], device_id=(other, me), device_id_type=MESH,
        ).wait_recv()
        sibling_copy(layer).wait_send()
    for side, there in sides:
        @pl.when(there)
        def _(side=side):
            offsets_copy(side).wait_send()
            for position in (0, 1):
                for layer in (0, 1):
                    window_copy(position, layer, side).wait_send()
            for s in range(4):
                update_copy(s, side).wait_send()
            for layer in (0, 1):
                for position in (0, 1):
                    pltpu.make_async_remote_copy(
                        src_ref=update.at[0, :, pl.ds(0, HALF)], dst_ref=grads.at[layer, 2 * side + position],
                        send_sem=out_send.at[side, 0], recv_sem=out_recv.at[layer, 2 * side + position],
                        device_id=(core, above if side == 0 else below), device_id_type=MESH,
                    ).wait_recv()


def place_kernel(width, offs, near_offs, grads, out):
    out[...] = jnp.zeros_like(out)
    row = lax.broadcasted_iota(jnp.int32, (HALF, HALF), 0)
    lane = lax.broadcasted_iota(jnp.int32, (HALF, HALF), 1)
    for window in range(6):
        side, position = window // 2, window % 2
        column = near_offs[side, position, 1] if side < 2 else offs[position, 1]
        block, shift = column_block(column, width)
        base = block * HALF
        value = grads[0, window, 0]
        if side == 0:
            value = jnp.where(jnp.concatenate([row, row], 1) < near_offs[0, position, 0], value, 0.0)
        elif side == 1:
            value = jnp.where(jnp.concatenate([row, row], 1) >= near_offs[1, position, 0], value, 0.0)
        mixed, pure = value[:, :HALF], value[:, HALF:]
        first = lane >= shift
        out[0, 0, :, pl.ds(pl.multiple_of(base, HALF), HALF)] += jnp.where(first, mixed, 0.0)
        out[0, 0, :, pl.ds(pl.multiple_of(base + HALF, HALF), HALF)] += pure
        out[0, 0, :, pl.ds(pl.multiple_of(base + 2 * HALF, HALF), HALF)] += jnp.where(first, 0.0, mixed)


def local(tiles, specimen, scan_offsets, probe_wave, fresnel_phase, measured):
    width = specimen.shape[3]
    any_space = pl.BlockSpec(memory_space=pl.ANY)
    smem = pl.BlockSpec(memory_space=pltpu.SMEM)
    dma = pltpu.SemaphoreType.DMA
    vm = lambda *shape: pltpu.VMEM(shape, F32)
    grads, near_offs = pl.pallas_call(
        functools.partial(main_kernel, tiles, width),
        out_shape=[
            jax.ShapeDtypeStruct((2, 6, 2, HALF, FULL), F32),
            jax.ShapeDtypeStruct((2, 2, 2), jnp.int32),
        ],
        in_specs=[smem] + [any_space] * 6,
        out_specs=[any_space, smem],
        scratch_shapes=[
            vm(2, 2, width // HALF, HALF, HALF),
            vm(2, FULL, FULL),
            vm(FULL, FULL),
            vm(FULL, FULL),
            pltpu.VMEM((4, 2, FULL, FULL), BF16),
            pltpu.VMEM((2, FULL, FULL), BF16),
            vm(2, 2, 2, 2, HALF, FULL),
            vm(2, 4, 2, HALF, FULL),
            vm(2, 2, HALF, FULL),
            vm(4, 2, HALF, FULL),
            vm(4, 2, FULL, FULL),
            vm(8, 2, FULL, FULL),
            vm(2, FULL, FULL),
            vm(2, FULL, FULL),
            vm(2, FULL, FULL),
            vm(4, 2, FULL, FULL),
            pltpu.SMEM((2, 2, 2), jnp.int32),
            dma((width // HALF,)), dma((5,)),
            dma((2,)), dma((2,)),
            dma((2, 2, 2)), dma((2, 4)),
            dma((2,)), dma((2,)),
            dma((2, 4)), dma((2, 4)),
            dma((2,)), dma((2,)), dma((2,)),
        ],
        compiler_params=pltpu.CompilerParams(
            collective_id=0, has_side_effects=True, vmem_limit_bytes=48 * 2**20
        ),
        name="ptycho",
    )(scan_offsets, specimen, probe_wave, fresnel_phase, measured, jnp.asarray(dft_tables()), jnp.asarray(order_tables()))
    return pl.pallas_call(
        functools.partial(place_kernel, width),
        out_shape=jax.ShapeDtypeStruct(specimen.shape, F32),
        grid=(2, 2),
        in_specs=[smem, smem, pl.BlockSpec((1, 6, 1, HALF, FULL), lambda s, c: (s, 0, c, 0, 0))],
        out_specs=pl.BlockSpec((1, 1, HALF, width), lambda s, c: (s, c, 0, 0)),
        name="place",
    )(scan_offsets, near_offs, grads)


def solution(mesh):
    placed = (P("depth", None, "tile", None), P("tile", None), P(), P(), P("tile", None, None))
    return jax.shard_map(
        functools.partial(local, mesh.shape["tile"]),
        mesh=mesh, in_specs=placed, out_specs=P("depth", None, "tile", None), check_vma=False,
    )
```

```python
import functools

import jax
import jax.numpy as jnp
import ml_dtypes
import numpy as np
from jax import lax
from jax.experimental import pallas as pl
from jax.experimental.pallas import tpu as pltpu
from jax.sharding import PartitionSpec as P

MESH = pl.DeviceIdType.MESH
F32 = jnp.float32
BF16 = jnp.bfloat16
HALF = 128
FULL = 256


def halves(matrix):
    high = matrix.astype(ml_dtypes.bfloat16)
    low = (matrix - high.astype(np.float64)).astype(ml_dtypes.bfloat16)
    return high, low


def dft_tables():
    n = np.arange(HALF)
    tables = []
    for parity in (0, 1):
        angle = 2.0 * np.pi * ((n[:, None] * (2 * n[None, :] + parity)) % FULL) / FULL
        cosine, sine = np.cos(angle) / 16.0, np.sin(angle) / 16.0
        right = np.block([[cosine, -sine], [sine, cosine]])
        tables.append(right)
    parts = [halves(m) for right in tables for m in (right, right.T)]
    return np.stack([np.stack(p) for p in parts])


def order_tables():
    order = np.concatenate([np.arange(0, FULL, 2), np.arange(1, FULL, 2)])
    right = np.zeros((FULL, FULL), np.float32)
    right[order, np.arange(FULL)] = 1.0
    return np.stack([right, right.T]).astype(ml_dtypes.bfloat16)


def dot(a, b):
    return jnp.dot(a, b, preferred_element_type=F32)


def two_parts(x):
    high = x.astype(BF16)
    low = (x - high.astype(F32)).astype(BF16)
    return high, low


def exact_right(x, ones):
    high = x.astype(BF16)
    rest = x - high.astype(F32)
    middle = rest.astype(BF16)
    low = (rest - middle.astype(F32)).astype(BF16)
    return (dot(high, ones) + dot(middle, ones)) + dot(low, ones)


def exact_left(ones, x):
    high = x.astype(BF16)
    rest = x - high.astype(F32)
    middle = rest.astype(BF16)
    low = (rest - middle.astype(F32)).astype(BF16)
    return (dot(ones, high) + dot(ones, middle)) + dot(ones, low)


def times_right(x, table):
    high, low = two_parts(x)
    return dot(high, table[0]) + (dot(low, table[0]) + dot(high, table[1]))


def times_left(table, x):
    high, low = two_parts(x)
    return dot(table[0], high) + (dot(table[0], low) + dot(table[1], high))


EVEN, EVEN_T, ODD, ODD_T = range(4)


def forward_transform(x_ref, z_ref, tab):
    re, im = x_ref[0], x_ref[1]
    even = jnp.concatenate([re[:, :HALF] + re[:, HALF:], im[:, :HALF] + im[:, HALF:]], 1)
    odd = jnp.concatenate([re[:, :HALF] - re[:, HALF:], im[:, :HALF] - im[:, HALF:]], 1)
    ye = times_right(even, tab.at[EVEN])
    yo = times_right(odd, tab.at[ODD])
    re = jnp.concatenate([ye[:, :HALF], yo[:, :HALF]], 1)
    im = jnp.concatenate([ye[:, HALF:], yo[:, HALF:]], 1)
    z_ref[0] = times_left(tab.at[EVEN_T], jnp.concatenate([re[:HALF] + re[HALF:], im[:HALF] + im[HALF:]], 0))
    z_ref[1] = times_left(tab.at[ODD_T], jnp.concatenate([re[:HALF] - re[HALF:], im[:HALF] - im[HALF:]], 0))


def inverse_transform(z_ref, out, tab):
    a = times_left(tab.at[EVEN], z_ref[0])
    b = times_left(tab.at[ODD], z_ref[1])
    total, rest = a + b, a - b
    re = jnp.concatenate([total[:HALF], rest[:HALF]], 0)
    im = jnp.concatenate([total[HALF:], rest[HALF:]], 0)
    a = times_right(jnp.concatenate([re[:, :HALF], im[:, :HALF]], 1), tab.at[EVEN_T])
    b = times_right(jnp.concatenate([re[:, HALF:], im[:, HALF:]], 1), tab.at[ODD_T])
    total, rest = a + b, a - b
    out[0] = jnp.concatenate([total[:, :HALF], rest[:, :HALF]], 1)
    out[1] = jnp.concatenate([total[:, HALF:], rest[:, HALF:]], 1)


def column_block(column, width):
    block = jnp.minimum(lax.shift_right_logical(column, 7), width // HALF - 3)
    return block, column - block * HALF


def take_window(spec, layer, component, column, width):
    block, shift = column_block(column, width)
    lane = lax.broadcasted_iota(jnp.int32, (HALF, HALF), 1)
    mixed = jnp.where(lane >= shift, spec[layer, component, block], spec[layer, component, block + 2])
    return mixed, spec[layer, component, block + 1]


def main_kernel(
    tiles, width,
    offs_hbm, spec_hbm, probe_hbm, phase_hbm, meas_hbm, tab_hbm, perm_hbm,
    grads, offs_out,
    offs, offs_table, spec, probe, phase, meas, tab, perm,
    staged, near, own_staged, own, patch, field, x_buf, z_buf, kern, update, offs_land,
    offs_sem, block_sem, load_sem, off_send, off_recv, in_send, in_recv, sib_send, sib_recv,
    out_send, out_recv, mid_send, mid_recv, mid_local,
):
    me = lax.axis_index("tile")
    core = lax.axis_index("depth")
    other = 1 - core
    has_above = me > 0
    has_below = me < tiles - 1
    above = jnp.maximum(me - 1, 0)
    below = jnp.minimum(me + 1, tiles - 1)

    barrier = pltpu.get_barrier_semaphore()
    pl.semaphore_signal(barrier, inc=1, device_id=(other, me), device_id_type=MESH)

    @pl.when(has_above)
    def _():
        for d in (0, 1):
            pl.semaphore_signal(barrier, inc=1, device_id=(d, above), device_id_type=MESH)

    @pl.when(has_below)
    def _():
        for d in (0, 1):
            pl.semaphore_signal(barrier, inc=1, device_id=(d, below), device_id_type=MESH)

    blocks = width // HALF

    def block_copy(b):
        return pltpu.make_async_copy(
            spec_hbm.at[:, :, :, pl.ds(b * HALF, HALF)], spec.at[:, :, b], block_sem.at[b]
        )

    loads = [
        pltpu.make_async_copy(tab_hbm, tab, load_sem.at[0]),
        pltpu.make_async_copy(perm_hbm, perm, load_sem.at[1]),
        pltpu.make_async_copy(probe_hbm, probe, load_sem.at[2]),
        pltpu.make_async_copy(phase_hbm, phase, load_sem.at[3]),
        pltpu.make_async_copy(meas_hbm.at[core], meas, load_sem.at[4]),
    ]
    offs_load = pltpu.make_async_copy(offs_hbm, offs, offs_sem.at[0])
    offs_store = pltpu.make_async_copy(offs_table, offs_out, offs_sem.at[1])
    offs_load.start()
    for b in range(blocks):
        block_copy(b).start()
    for copy in loads:
        copy.start()
    offs_load.wait()
    pl.semaphore_wait(barrier, 1 + 2 * has_above.astype(jnp.int32) + 2 * has_below.astype(jnp.int32))

    def offsets_copy(side):
        return pltpu.make_async_remote_copy(
            src_ref=offs, dst_ref=offs_land.at[1 - side], send_sem=off_send.at[side], recv_sem=off_recv.at[1 - side],
            device_id=(core, above if side == 0 else below), device_id_type=MESH,
        )

    sides = ((0, has_above), (1, has_below))
    for side, there in sides:
        pl.when(there)(offsets_copy(side).start)

    for b in range(blocks):
        block_copy(b).wait()
    for layer in (0, 1):
        for c in (0, 1):
            mixed, pure = take_window(spec, layer, c, offs[other, 1], width)
            own_staged[layer, c, :, :HALF] = mixed
            own_staged[layer, c, :, HALF:] = pure

    def sibling_copy(layer):
        return pltpu.make_async_remote_copy(
            src_ref=own_staged.at[layer], dst_ref=own.at[2 * core + layer], send_sem=sib_send.at[layer],
            recv_sem=sib_recv.at[layer], device_id=(other, me), device_id_type=MESH,
        )

    for layer in (0, 1):
        sibling_copy(layer).start()
    for layer in (0, 1):
        for c in (0, 1):
            mixed, pure = take_window(spec, layer, c, offs[core, 1], width)
            own[2 * core + layer, c, :, :HALF] = mixed
            own[2 * core + layer, c, :, HALF:] = pure

    def window_copy(position, layer, side):
        return pltpu.make_async_remote_copy(
            src_ref=staged.at[side, position, layer], dst_ref=near.at[1 - side, 2 * core + layer],
            send_sem=in_send.at[side, position, layer], recv_sem=in_recv.at[1 - side, 2 * core + layer],
            device_id=(position, above if side == 0 else below), device_id_type=MESH,
        )

    for side, there in sides:
        @pl.when(there)
        def _(side=side):
            pltpu.make_async_remote_copy(
                src_ref=offs, dst_ref=offs_land.at[side], send_sem=off_send.at[side], recv_sem=off_recv.at[side],
                device_id=(core, above if side == 0 else below), device_id_type=MESH,
            ).wait_recv()

    for position in (0, 1):
        for layer in (0, 1):
            for side, there in sides:
                @pl.when(there)
                def _(position=position, layer=layer, side=side):
                    for c in (0, 1):
                        mixed, pure = take_window(spec, layer, c, offs_land[side, position, 1], width)
                        staged[side, position, layer, c, :, :HALF] = mixed
                        staged[side, position, layer, c, :, HALF:] = pure
                    window_copy(position, layer, side).start()

    for side, there in sides:
        for position in (0, 1):
            first = offs_land[side, position, 0] - (me - 2 + 2 * side) * HALF
            offs_table[side, position, 0] = jnp.where(there, first, HALF * side)
            offs_table[side, position, 1] = jnp.where(there, offs_land[side, position, 1], 0)
    for position in (0, 1):
        offs_table[2, position, 0] = 0
        offs_table[2, position, 1] = offs[position, 1]
    offs_store.start()

    first = offs[core, 0] - (me - 1) * HALF
    unused, shift = column_block(offs[core, 1], width)
    for copy in loads:
        copy.wait()
    phases = exact_right(exact_left(perm[1], phase[...]), perm[0])
    kern[0] = jnp.cos(phases)
    kern[1] = jnp.sin(phases)
    meas[...] = exact_right(exact_left(perm[1], meas[...]), perm[0])
    rows = lax.broadcasted_iota(jnp.int32, (FULL, FULL), 0)
    cols = lax.broadcasted_iota(jnp.int32, (FULL, FULL), 1)
    turn = jnp.where(((cols + first) & (FULL - 1)) == rows, 1.0, 0.0).astype(BF16)
    slide = jnp.where(((rows + shift) & (FULL - 1)) == cols, 1.0, 0.0).astype(BF16)
    for c in (0, 1):
        field[0, c] = exact_right(exact_left(turn, probe[c]), slide)

    for layer in (0, 1):
        pltpu.make_async_remote_copy(
            src_ref=own_staged.at[layer], dst_ref=own.at[2 * other + layer], send_sem=sib_send.at[layer],
            recv_sem=sib_recv.at[layer], device_id=(other, me), device_id_type=MESH,
        ).wait_recv()

    half_rows = lax.broadcasted_iota(jnp.int32, (HALF, FULL), 0)

    def update_copy(s, side):
        target = s // 2
        return pltpu.make_async_remote_copy(
            src_ref=update.at[s, :, pl.ds(0, HALF)], dst_ref=grads.at[s - 2 * target, 2 * (1 - side) + core],
            send_sem=out_send.at[side, s], recv_sem=out_recv.at[s - 2 * target, 2 * (1 - side) + core],
            device_id=(target, above if side == 0 else below), device_id_type=MESH,
        )

    def middle_copy(layer):
        return pltpu.make_async_remote_copy(
            src_ref=update.at[2 * other + layer, :, pl.ds(HALF, HALF)], dst_ref=grads.at[layer, 4 + core],
            send_sem=mid_send.at[layer], recv_sem=mid_recv.at[layer], device_id=(other, me), device_id_type=MESH,
        )

    def middle_local(layer):
        return pltpu.make_async_copy(
            update.at[2 * core + layer, :, pl.ds(HALF, HALF)], grads.at[layer, 4 + core], mid_local.at[layer]
        )

    def step(i, carry):
        @pl.when(i <= 3)
        def _():
            for side, there in sides:
                @pl.when(there)
                def _(side=side):
                    pltpu.make_async_remote_copy(
                        src_ref=staged.at[side, 0, 0], dst_ref=near.at[side, i], send_sem=in_send.at[side, 0, 0],
                        recv_sem=in_recv.at[side, i], device_id=(core, above if side == 0 else below),
                        device_id_type=MESH,
                    ).wait_recv()
            top = [jnp.where(half_rows >= first, near[0, i, c], near[1, i, c]) for c in (0, 1)]
            bottom = [own[i, c] for c in (0, 1)]
            for c in (0, 1):
                patch[i, c, :HALF] = top[c]
                patch[i, c, HALF:] = bottom[c]
            for part, (pr, pi) in enumerate((top, bottom)):
                span = pl.ds(part * HALF, HALF)
                wr, wi = field[i, 0, span], field[i, 1, span]
                x_buf[0, span] = wr * pr - wi * pi
                x_buf[1, span] = wr * pi + wi * pr

        @pl.when(i > 3)
        def _():
            pr, pi = patch[7 - i, 0], patch[7 - i, 1]
            ar, ai = field[i, 0], field[i, 1]
            x_buf[0] = pr * ar + pi * ai
            x_buf[1] = pr * ai - pi * ar

        forward_transform(x_buf, z_buf, tab)

        @pl.when(i == 3)
        def _():
            for parity in (0, 1):
                zr, zi = z_buf[parity, :HALF], z_buf[parity, HALF:]
                e = 2.0 * (zr * zr + zi * zi - meas[parity * HALF : (parity + 1) * HALF])
                z_buf[parity, :HALF] = e * zr
                z_buf[parity, HALF:] = e * zi

        @pl.when(i != 3)
        def _():
            sign = jnp.where(i < 3, 1.0, -1.0)
            for parity in (0, 1):
                span = slice(parity * HALF, (parity + 1) * HALF)
                zr, zi = z_buf[parity, :HALF], z_buf[parity, HALF:]
                kr, ki = kern[0, span], sign * kern[1, span]
                z_buf[parity, :HALF] = kr * zr - ki * zi
                z_buf[parity, HALF:] = kr * zi + ki * zr

        inverse_transform(z_buf, field.at[i + 1], tab)

        @pl.when(i >= 3)
        def _():
            s = 6 - i
            wr, wi = field[s, 0], field[s, 1]
            ar, ai = field[i + 1, 0], field[i + 1, 1]
            update[s, 0] = wr * ar + wi * ai
            update[s, 1] = wr * ai - wi * ar
            for side, there in sides:
                @pl.when(there)
                def _(side=side):
                    update_copy(s, side).start()
            for layer in (0, 1):
                pl.when(s == 2 * other + layer)(middle_copy(layer).start)
                pl.when(s == 2 * core + layer)(middle_local(layer).start)

        return carry

    lax.fori_loop(0, 7, step, 0)

    offs_store.wait()
    for layer in (0, 1):
        middle_local(layer).wait()
        middle_copy(layer).wait_send()
        pltpu.make_async_remote_copy(
            src_ref=update.at[0, :, pl.ds(HALF, HALF)], dst_ref=grads.at[layer, 4 + other],
            send_sem=mid_send.at[layer], recv_sem=mid_recv.at[layer], device_id=(other, me), device_id_type=MESH,
        ).wait_recv()
        sibling_copy(layer).wait_send()
    for side, there in sides:
        @pl.when(there)
        def _(side=side):
            offsets_copy(side).wait_send()
            for position in (0, 1):
                for layer in (0, 1):
                    window_copy(position, layer, side).wait_send()
            for s in range(4):
                update_copy(s, side).wait_send()
            for layer in (0, 1):
                for position in (0, 1):
                    pltpu.make_async_remote_copy(
                        src_ref=update.at[0, :, pl.ds(0, HALF)], dst_ref=grads.at[layer, 2 * side + position],
                        send_sem=out_send.at[side, 0], recv_sem=out_recv.at[layer, 2 * side + position],
                        device_id=(core, above if side == 0 else below), device_id_type=MESH,
                    ).wait_recv()


def place_kernel(width, offs_hbm, grads, out, offs, held, strip, offs_sem, in_sem, out_sem):
    def in_copy(layer, c):
        return pltpu.make_async_copy(grads.at[layer, :, c], held.at[layer, c], in_sem.at[layer, c])

    def out_copy(layer, c):
        return pltpu.make_async_copy(strip.at[layer, c], out.at[layer, c], out_sem.at[layer, c])

    parts = [(layer, c) for layer in (0, 1) for c in (0, 1)]
    offs_load = pltpu.make_async_copy(offs_hbm, offs, offs_sem)
    offs_load.start()
    for part in parts:
        in_copy(*part).start()
    strip[...] = jnp.zeros_like(strip)
    row = lax.broadcasted_iota(jnp.int32, (HALF, FULL), 0)
    lane = lax.broadcasted_iota(jnp.int32, (HALF, HALF), 1)
    offs_load.wait()
    for layer, c in parts:
        in_copy(layer, c).wait()
        for window in range(6):
            side, position = window // 2, window % 2
            block, shift = column_block(offs[side, position, 1], width)
            value = held[layer, c, window]
            if side == 0:
                value = jnp.where(row < offs[0, position, 0], value, 0.0)
            elif side == 1:
                value = jnp.where(row >= offs[1, position, 0], value, 0.0)
            mixed, pure = value[:, :HALF], value[:, HALF:]
            first = lane >= shift
            for k, piece in enumerate((jnp.where(first, mixed, 0.0), pure, jnp.where(first, 0.0, mixed))):
                span = pl.ds(pl.multiple_of((block + k) * HALF, HALF), HALF)
                strip[layer, c, :, span] += piece
        out_copy(layer, c).start()
    for part in parts:
        out_copy(*part).wait()


def local(tiles, specimen, scan_offsets, probe_wave, fresnel_phase, measured):
    width = specimen.shape[3]
    any_space = pl.BlockSpec(memory_space=pl.ANY)
    dma = pltpu.SemaphoreType.DMA
    vm = lambda *shape: pltpu.VMEM(shape, F32)
    grads, near_offs = pl.pallas_call(
        functools.partial(main_kernel, tiles, width),
        out_shape=[
            jax.ShapeDtypeStruct((2, 6, 2, HALF, FULL), F32),
            jax.ShapeDtypeStruct((3, 2, 2), jnp.int32),
        ],
        in_specs=[any_space] * 7,
        out_specs=[any_space, any_space],
        scratch_shapes=[
            pltpu.SMEM((2, 2), jnp.int32),
            pltpu.SMEM((3, 2, 2), jnp.int32),
            vm(2, 2, width // HALF, HALF, HALF),
            vm(2, FULL, FULL),
            vm(FULL, FULL),
            vm(FULL, FULL),
            pltpu.VMEM((4, 2, FULL, FULL), BF16),
            pltpu.VMEM((2, FULL, FULL), BF16),
            vm(2, 2, 2, 2, HALF, FULL),
            vm(2, 4, 2, HALF, FULL),
            vm(2, 2, HALF, FULL),
            vm(4, 2, HALF, FULL),
            vm(4, 2, FULL, FULL),
            vm(8, 2, FULL, FULL),
            vm(2, FULL, FULL),
            vm(2, FULL, FULL),
            vm(2, FULL, FULL),
            vm(4, 2, FULL, FULL),
            pltpu.SMEM((2, 2, 2), jnp.int32),
            dma((2,)), dma((width // HALF,)), dma((5,)),
            dma((2,)), dma((2,)),
            dma((2, 2, 2)), dma((2, 4)),
            dma((2,)), dma((2,)),
            dma((2, 4)), dma((2, 4)),
            dma((2,)), dma((2,)), dma((2,)),
        ],
        compiler_params=pltpu.CompilerParams(
            collective_id=0, has_side_effects=True, vmem_limit_bytes=60 * 2**20
        ),
        name="ptycho",
    )(scan_offsets, specimen, probe_wave, fresnel_phase, measured, jnp.asarray(dft_tables()), jnp.asarray(order_tables()))
    return pl.pallas_call(
        functools.partial(place_kernel, width),
        out_shape=jax.ShapeDtypeStruct(specimen.shape, F32),
        in_specs=[any_space, any_space],
        out_specs=any_space,
        scratch_shapes=[
            pltpu.SMEM((3, 2, 2), jnp.int32), vm(2, 2, 6, HALF, FULL), vm(2, 2, HALF, width),
            dma, dma((2, 2)), dma((2, 2)),
        ],
        compiler_params=pltpu.CompilerParams(vmem_limit_bytes=60 * 2**20),
        name="place",
    )(near_offs, grads)


def solution(mesh):
    placed = (P("depth", None, "tile", None), P("tile", None), P(), P(), P("tile", None, None))
    return jax.shard_map(
        functools.partial(local, mesh.shape["tile"]),
        mesh=mesh, in_specs=placed, out_specs=P("depth", None, "tile", None), check_vma=False,
    )
```

```python
import functools

import jax
import jax.numpy as jnp
import ml_dtypes
import numpy as np
from jax import lax
from jax.experimental import pallas as pl
from jax.experimental.pallas import tpu as pltpu
from jax.sharding import PartitionSpec as P

MESH = pl.DeviceIdType.MESH
F32 = jnp.float32
BF16 = jnp.bfloat16
HALF = 128
FULL = 256
RING = 4


def halves(matrix):
    high = matrix.astype(ml_dtypes.bfloat16)
    low = (matrix - high.astype(np.float64)).astype(ml_dtypes.bfloat16)
    return high, low


def dft_tables():
    n = np.arange(HALF)
    tables = []
    for parity in (0, 1):
        angle = 2.0 * np.pi * ((n[:, None] * (2 * n[None, :] + parity)) % FULL) / FULL
        cosine, sine = np.cos(angle) / 16.0, np.sin(angle) / 16.0
        right = np.block([[cosine, -sine], [sine, cosine]])
        tables.append(right)
    parts = [halves(m) for right in tables for m in (right, right.T)]
    return np.stack([np.stack(p) for p in parts])


def order_tables():
    order = np.concatenate([np.arange(0, FULL, 2), np.arange(1, FULL, 2)])
    right = np.zeros((FULL, FULL), np.float32)
    right[order, np.arange(FULL)] = 1.0
    return np.stack([right, right.T]).astype(ml_dtypes.bfloat16)


def dot(a, b):
    return jnp.dot(a, b, preferred_element_type=F32)


def two_parts(x):
    high = x.astype(BF16)
    low = (x - high.astype(F32)).astype(BF16)
    return high, low


def exact_right(x, ones):
    high = x.astype(BF16)
    rest = x - high.astype(F32)
    middle = rest.astype(BF16)
    low = (rest - middle.astype(F32)).astype(BF16)
    return (dot(high, ones) + dot(middle, ones)) + dot(low, ones)


def exact_left(ones, x):
    high = x.astype(BF16)
    rest = x - high.astype(F32)
    middle = rest.astype(BF16)
    low = (rest - middle.astype(F32)).astype(BF16)
    return (dot(ones, high) + dot(ones, middle)) + dot(ones, low)


def times_right(x, table):
    high, low = two_parts(x)
    return dot(high, table[0]) + (dot(low, table[0]) + dot(high, table[1]))


def times_left(table, x):
    high, low = two_parts(x)
    return dot(table[0], high) + (dot(table[0], low) + dot(table[1], high))


EVEN, EVEN_T, ODD, ODD_T = range(4)


def forward_transform(x_ref, z_ref, tab):
    re, im = x_ref[0], x_ref[1]
    even = jnp.concatenate([re[:, :HALF] + re[:, HALF:], im[:, :HALF] + im[:, HALF:]], 1)
    odd = jnp.concatenate([re[:, :HALF] - re[:, HALF:], im[:, :HALF] - im[:, HALF:]], 1)
    ye = times_right(even, tab.at[EVEN])
    yo = times_right(odd, tab.at[ODD])
    re = jnp.concatenate([ye[:, :HALF], yo[:, :HALF]], 1)
    im = jnp.concatenate([ye[:, HALF:], yo[:, HALF:]], 1)
    z_ref[0] = times_left(tab.at[EVEN_T], jnp.concatenate([re[:HALF] + re[HALF:], im[:HALF] + im[HALF:]], 0))
    z_ref[1] = times_left(tab.at[ODD_T], jnp.concatenate([re[:HALF] - re[HALF:], im[:HALF] - im[HALF:]], 0))


def inverse_transform(z_ref, out, tab):
    a = times_left(tab.at[EVEN], z_ref[0])
    b = times_left(tab.at[ODD], z_ref[1])
    total, rest = a + b, a - b
    re = jnp.concatenate([total[:HALF], rest[:HALF]], 0)
    im = jnp.concatenate([total[HALF:], rest[HALF:]], 0)
    a = times_right(jnp.concatenate([re[:, :HALF], im[:, :HALF]], 1), tab.at[EVEN_T])
    b = times_right(jnp.concatenate([re[:, HALF:], im[:, HALF:]], 1), tab.at[ODD_T])
    total, rest = a + b, a - b
    out[0] = jnp.concatenate([total[:, :HALF], rest[:, :HALF]], 1)
    out[1] = jnp.concatenate([total[:, HALF:], rest[:, HALF:]], 1)


def column_block(column, width):
    block = jnp.minimum(lax.shift_right_logical(column, 7), width // HALF - 3)
    return block, column - block * HALF


def take_window(spec, layer, component, column, width):
    block, shift = column_block(column, width)
    lane = lax.broadcasted_iota(jnp.int32, (HALF, HALF), 1)
    mixed = jnp.where(lane >= shift, spec[layer, component, block], spec[layer, component, block + 2])
    return mixed, spec[layer, component, block + 1]


def main_kernel(
    tiles, width,
    offs_hbm, spec_hbm, probe_hbm, phase_hbm, meas_hbm, tab_hbm, perm_hbm,
    grads, offs_out,
    offs, offs_table, spec, probe, phase, meas, tab, perm,
    staged, near, own_staged, own, patch, field, x_buf, z_buf, kern, update, relayed, offs_land,
    offs_sem, block_sem, load_sem, off_send, off_recv, in_send, in_recv, sib_send, sib_recv,
    out_send, out_recv, mid_send, mid_recv, mid_local, relay_send, relay_recv, relay_ready,
):
    me = lax.axis_index("tile")
    core = lax.axis_index("depth")
    other = 1 - core
    has_above = me > 0
    has_below = me < tiles - 1
    above = jnp.maximum(me - 1, 0)
    below = jnp.minimum(me + 1, tiles - 1)

    place = lax.rem(me, RING * RING)
    far_source = (place == RING * RING - 1) & has_below & (core == 1)
    relays = (place == RING * RING - 3) & (me + 3 < tiles) & (core == 1)
    far_target = (place == 0) & has_above & (core == 1)

    def tile_at(distance):
        return jnp.clip(me + distance, 0, tiles - 1)

    barrier = pltpu.get_barrier_semaphore()
    pl.semaphore_signal(barrier, inc=1, device_id=(other, me), device_id_type=MESH)

    @pl.when(has_above)
    def _():
        for d in (0, 1):
            pl.semaphore_signal(barrier, inc=1, device_id=(d, above), device_id_type=MESH)

    @pl.when(has_below)
    def _():
        for d in (0, 1):
            pl.semaphore_signal(barrier, inc=1, device_id=(d, below), device_id_type=MESH)

    @pl.when(relays)
    def _():
        pl.semaphore_signal(barrier, inc=1, device_id=(core, tile_at(2)), device_id_type=MESH)
        pl.semaphore_signal(barrier, inc=1, device_id=(core, tile_at(3)), device_id_type=MESH)

    blocks = width // HALF

    def block_copy(b):
        return pltpu.make_async_copy(
            spec_hbm.at[:, :, :, pl.ds(b * HALF, HALF)], spec.at[:, :, b], block_sem.at[b]
        )

    loads = [
        pltpu.make_async_copy(tab_hbm, tab, load_sem.at[0]),
        pltpu.make_async_copy(perm_hbm, perm, load_sem.at[1]),
        pltpu.make_async_copy(probe_hbm, probe, load_sem.at[2]),
        pltpu.make_async_copy(phase_hbm, phase, load_sem.at[3]),
        pltpu.make_async_copy(meas_hbm.at[core], meas, load_sem.at[4]),
    ]
    offs_load = pltpu.make_async_copy(offs_hbm, offs, offs_sem.at[0])
    offs_store = pltpu.make_async_copy(offs_table, offs_out, offs_sem.at[1])
    offs_load.start()
    for b in range(blocks):
        block_copy(b).start()
    for copy in loads:
        copy.start()
    offs_load.wait()
    present = 1 + 2 * has_above.astype(jnp.int32) + 2 * has_below.astype(jnp.int32)
    pl.semaphore_wait(barrier, present + (far_source | far_target).astype(jnp.int32))

    def offsets_copy(side):
        return pltpu.make_async_remote_copy(
            src_ref=offs, dst_ref=offs_land.at[1 - side], send_sem=off_send.at[side], recv_sem=off_recv.at[1 - side],
            device_id=(core, above if side == 0 else below), device_id_type=MESH,
        )

    sides = ((0, has_above), (1, has_below))
    for side, there in sides:
        pl.when(there)(offsets_copy(side).start)

    @pl.when(far_target)
    def _():
        pl.semaphore_signal(relay_ready, inc=1, device_id=(core, tile_at(-3)), device_id_type=MESH)

    for b in range(blocks):
        block_copy(b).wait()
    for layer in (0, 1):
        for c in (0, 1):
            mixed, pure = take_window(spec, layer, c, offs[other, 1], width)
            own_staged[layer, c, :, :HALF] = mixed
            own_staged[layer, c, :, HALF:] = pure

    def sibling_copy(layer):
        return pltpu.make_async_remote_copy(
            src_ref=own_staged.at[layer], dst_ref=own.at[2 * core + layer], send_sem=sib_send.at[layer],
            recv_sem=sib_recv.at[layer], device_id=(other, me), device_id_type=MESH,
        )

    for layer in (0, 1):
        sibling_copy(layer).start()
    for layer in (0, 1):
        for c in (0, 1):
            mixed, pure = take_window(spec, layer, c, offs[core, 1], width)
            own[2 * core + layer, c, :, :HALF] = mixed
            own[2 * core + layer, c, :, HALF:] = pure

    def window_copy(position, layer, side):
        return pltpu.make_async_remote_copy(
            src_ref=staged.at[side, position, layer], dst_ref=near.at[1 - side, 2 * core + layer],
            send_sem=in_send.at[side, position, layer], recv_sem=in_recv.at[1 - side, 2 * core + layer],
            device_id=(position, above if side == 0 else below), device_id_type=MESH,
        )

    def detour_copy():
        return pltpu.make_async_remote_copy(
            src_ref=staged.at[1, 1, 1], dst_ref=relayed, send_sem=in_send.at[1, 1, 1], recv_sem=relay_recv,
            device_id=(core, tile_at(-2)), device_id_type=MESH,
        )

    def relay_copy():
        return pltpu.make_async_remote_copy(
            src_ref=relayed, dst_ref=near.at[0, 3], send_sem=relay_send, recv_sem=in_recv.at[0, 3],
            device_id=(core, tile_at(3)), device_id_type=MESH,
        )

    def wait_offsets(side):
        pltpu.make_async_remote_copy(
            src_ref=offs, dst_ref=offs_land.at[side], send_sem=off_send.at[side], recv_sem=off_recv.at[side],
            device_id=(core, above if side == 0 else below), device_id_type=MESH,
        ).wait_recv()

    def cut(side, position, layer):
        for c in (0, 1):
            mixed, pure = take_window(spec, layer, c, offs_land[side, position, 1], width)
            staged[side, position, layer, c, :, :HALF] = mixed
            staged[side, position, layer, c, :, HALF:] = pure

    def send(side, position, layer):
        cut(side, position, layer)
        window_copy(position, layer, side).start()

    def answer(side):
        wait_offsets(side)
        for position in (0, 1):
            for layer in (0, 1):
                send(side, position, layer)

    first_of_ring = lax.rem(me, RING) == 0
    usual = jnp.logical_not(far_source)
    pl.when(has_above & jnp.logical_not(first_of_ring) & usual)(functools.partial(answer, 0))
    pl.when(has_below & usual)(functools.partial(answer, 1))
    pl.when(has_above & first_of_ring & usual)(functools.partial(answer, 0))

    @pl.when(far_source)
    def _():
        wait_offsets(0)
        send(0, 0, 0)
        send(0, 0, 1)
        wait_offsets(1)
        cut(1, 1, 1)
        detour_copy().start()
        for side, position, layer in ((1, 0, 0), (0, 1, 0), (1, 0, 1), (0, 1, 1), (1, 1, 0)):
            send(side, position, layer)

    for side, there in sides:
        for position in (0, 1):
            first = offs_land[side, position, 0] - (me - 2 + 2 * side) * HALF
            offs_table[side, position, 0] = jnp.where(there, first, HALF * side)
            offs_table[side, position, 1] = jnp.where(there, offs_land[side, position, 1], 0)
    for position in (0, 1):
        offs_table[2, position, 0] = 0
        offs_table[2, position, 1] = offs[position, 1]
    offs_store.start()

    first = offs[core, 0] - (me - 1) * HALF
    unused, shift = column_block(offs[core, 1], width)
    for copy in loads:
        copy.wait()
    phases = exact_right(exact_left(perm[1], phase[...]), perm[0])
    kern[0] = jnp.cos(phases)
    kern[1] = jnp.sin(phases)
    meas[...] = exact_right(exact_left(perm[1], meas[...]), perm[0])
    rows = lax.broadcasted_iota(jnp.int32, (FULL, FULL), 0)
    cols = lax.broadcasted_iota(jnp.int32, (FULL, FULL), 1)
    turn = jnp.where(((cols + first) & (FULL - 1)) == rows, 1.0, 0.0).astype(BF16)
    slide = jnp.where(((rows + shift) & (FULL - 1)) == cols, 1.0, 0.0).astype(BF16)
    for c in (0, 1):
        field[0, c] = exact_right(exact_left(turn, probe[c]), slide)

    for layer in (0, 1):
        pltpu.make_async_remote_copy(
            src_ref=own_staged.at[layer], dst_ref=own.at[2 * other + layer], send_sem=sib_send.at[layer],
            recv_sem=sib_recv.at[layer], device_id=(other, me), device_id_type=MESH,
        ).wait_recv()

    half_rows = lax.broadcasted_iota(jnp.int32, (HALF, FULL), 0)

    def update_copy(s, side):
        target = s // 2
        return pltpu.make_async_remote_copy(
            src_ref=update.at[s, :, pl.ds(0, HALF)], dst_ref=grads.at[s - 2 * target, 2 * (1 - side) + core],
            send_sem=out_send.at[side, s], recv_sem=out_recv.at[s - 2 * target, 2 * (1 - side) + core],
            device_id=(target, above if side == 0 else below), device_id_type=MESH,
        )

    def middle_copy(layer):
        return pltpu.make_async_remote_copy(
            src_ref=update.at[2 * other + layer, :, pl.ds(HALF, HALF)], dst_ref=grads.at[layer, 4 + core],
            send_sem=mid_send.at[layer], recv_sem=mid_recv.at[layer], device_id=(other, me), device_id_type=MESH,
        )

    def middle_local(layer):
        return pltpu.make_async_copy(
            update.at[2 * core + layer, :, pl.ds(HALF, HALF)], grads.at[layer, 4 + core], mid_local.at[layer]
        )

    def step(i, carry):
        @pl.when(i <= 3)
        def _():
            for side, there in sides:
                @pl.when(there)
                def _(side=side):
                    pltpu.make_async_remote_copy(
                        src_ref=staged.at[side, 0, 0], dst_ref=near.at[side, i], send_sem=in_send.at[side, 0, 0],
                        recv_sem=in_recv.at[side, i], device_id=(core, above if side == 0 else below),
                        device_id_type=MESH,
                    ).wait_recv()
            top = [jnp.where(half_rows >= first, near[0, i, c], near[1, i, c]) for c in (0, 1)]
            bottom = [own[i, c] for c in (0, 1)]
            for c in (0, 1):
                patch[i, c, :HALF] = top[c]
                patch[i, c, HALF:] = bottom[c]
            for part, (pr, pi) in enumerate((top, bottom)):
                span = pl.ds(part * HALF, HALF)
                wr, wi = field[i, 0, span], field[i, 1, span]
                x_buf[0, span] = wr * pr - wi * pi
                x_buf[1, span] = wr * pi + wi * pr

        @pl.when(i > 3)
        def _():
            pr, pi = patch[7 - i, 0], patch[7 - i, 1]
            ar, ai = field[i, 0], field[i, 1]
            x_buf[0] = pr * ar + pi * ai
            x_buf[1] = pr * ai - pi * ar

        @pl.when(relays & (i == 1))
        def _():
            pl.semaphore_wait(relay_ready, 1)
            pltpu.make_async_remote_copy(
                src_ref=relayed, dst_ref=relayed, send_sem=relay_send, recv_sem=relay_recv,
                device_id=(core, tile_at(2)), device_id_type=MESH,
            ).wait_recv()
            relay_copy().start()

        forward_transform(x_buf, z_buf, tab)

        @pl.when(i == 3)
        def _():
            for parity in (0, 1):
                zr, zi = z_buf[parity, :HALF], z_buf[parity, HALF:]
                e = 2.0 * (zr * zr + zi * zi - meas[parity * HALF : (parity + 1) * HALF])
                z_buf[parity, :HALF] = e * zr
                z_buf[parity, HALF:] = e * zi

        @pl.when(i != 3)
        def _():
            sign = jnp.where(i < 3, 1.0, -1.0)
            for parity in (0, 1):
                span = slice(parity * HALF, (parity + 1) * HALF)
                zr, zi = z_buf[parity, :HALF], z_buf[parity, HALF:]
                kr, ki = kern[0, span], sign * kern[1, span]
                z_buf[parity, :HALF] = kr * zr - ki * zi
                z_buf[parity, HALF:] = kr * zi + ki * zr

        inverse_transform(z_buf, field.at[i + 1], tab)

        @pl.when(i >= 3)
        def _():
            s = 6 - i
            wr, wi = field[s, 0], field[s, 1]
            ar, ai = field[i + 1, 0], field[i + 1, 1]
            update[s, 0] = wr * ar + wi * ai
            update[s, 1] = wr * ai - wi * ar
            for side, there in sides:
                @pl.when(there)
                def _(side=side):
                    update_copy(s, side).start()
            for layer in (0, 1):
                pl.when(s == 2 * other + layer)(middle_copy(layer).start)
                pl.when(s == 2 * core + layer)(middle_local(layer).start)

        return carry

    lax.fori_loop(0, 7, step, 0)

    offs_store.wait()
    pl.when(relays)(relay_copy().wait_send)
    for layer in (0, 1):
        middle_local(layer).wait()
        middle_copy(layer).wait_send()
        pltpu.make_async_remote_copy(
            src_ref=update.at[0, :, pl.ds(HALF, HALF)], dst_ref=grads.at[layer, 4 + other],
            send_sem=mid_send.at[layer], recv_sem=mid_recv.at[layer], device_id=(other, me), device_id_type=MESH,
        ).wait_recv()
        sibling_copy(layer).wait_send()
    for side, there in sides:
        @pl.when(there)
        def _(side=side):
            offsets_copy(side).wait_send()
            for position in (0, 1):
                for layer in (0, 1):
                    window_copy(position, layer, side).wait_send()
            for s in range(4):
                update_copy(s, side).wait_send()
            for layer in (0, 1):
                for position in (0, 1):
                    pltpu.make_async_remote_copy(
                        src_ref=update.at[0, :, pl.ds(0, HALF)], dst_ref=grads.at[layer, 2 * side + position],
                        send_sem=out_send.at[side, 0], recv_sem=out_recv.at[layer, 2 * side + position],
                        device_id=(core, above if side == 0 else below), device_id_type=MESH,
                    ).wait_recv()


def place_kernel(width, offs_hbm, grads, out, offs, held, strip, offs_sem, in_sem, out_sem):
    def in_copy(layer, c):
        return pltpu.make_async_copy(grads.at[layer, :, c], held.at[layer, c], in_sem.at[layer, c])

    def out_copy(layer, c):
        return pltpu.make_async_copy(strip.at[layer, c], out.at[layer, c], out_sem.at[layer, c])

    parts = [(layer, c) for layer in (0, 1) for c in (0, 1)]
    offs_load = pltpu.make_async_copy(offs_hbm, offs, offs_sem)
    offs_load.start()
    for part in parts:
        in_copy(*part).start()
    strip[...] = jnp.zeros_like(strip)
    row = lax.broadcasted_iota(jnp.int32, (HALF, FULL), 0)
    lane = lax.broadcasted_iota(jnp.int32, (HALF, HALF), 1)
    offs_load.wait()
    for layer, c in parts:
        in_copy(layer, c).wait()
        for window in range(6):
            side, position = window // 2, window % 2
            block, shift = column_block(offs[side, position, 1], width)
            value = held[layer, c, window]
            if side == 0:
                value = jnp.where(row < offs[0, position, 0], value, 0.0)
            elif side == 1:
                value = jnp.where(row >= offs[1, position, 0], value, 0.0)
            mixed, pure = value[:, :HALF], value[:, HALF:]
            first = lane >= shift
            for k, piece in enumerate((jnp.where(first, mixed, 0.0), pure, jnp.where(first, 0.0, mixed))):
                span = pl.ds(pl.multiple_of((block + k) * HALF, HALF), HALF)
                strip[layer, c, :, span] += piece
        out_copy(layer, c).start()
    for part in parts:
        out_copy(*part).wait()


def local(tiles, specimen, scan_offsets, probe_wave, fresnel_phase, measured):
    width = specimen.shape[3]
    any_space = pl.BlockSpec(memory_space=pl.ANY)
    dma = pltpu.SemaphoreType.DMA
    vm = lambda *shape: pltpu.VMEM(shape, F32)
    grads, near_offs = pl.pallas_call(
        functools.partial(main_kernel, tiles, width),
        out_shape=[
            jax.ShapeDtypeStruct((2, 6, 2, HALF, FULL), F32),
            jax.ShapeDtypeStruct((3, 2, 2), jnp.int32),
        ],
        in_specs=[any_space] * 7,
        out_specs=[any_space, any_space],
        scratch_shapes=[
            pltpu.SMEM((2, 2), jnp.int32),
            pltpu.SMEM((3, 2, 2), jnp.int32),
            vm(2, 2, width // HALF, HALF, HALF),
            vm(2, FULL, FULL),
            vm(FULL, FULL),
            vm(FULL, FULL),
            pltpu.VMEM((4, 2, FULL, FULL), BF16),
            pltpu.VMEM((2, FULL, FULL), BF16),
            vm(2, 2, 2, 2, HALF, FULL),
            vm(2, 4, 2, HALF, FULL),
            vm(2, 2, HALF, FULL),
            vm(4, 2, HALF, FULL),
            vm(4, 2, FULL, FULL),
            vm(8, 2, FULL, FULL),
            vm(2, FULL, FULL),
            vm(2, FULL, FULL),
            vm(2, FULL, FULL),
            vm(4, 2, FULL, FULL),
            vm(2, HALF, FULL),
            pltpu.SMEM((2, 2, 2), jnp.int32),
            dma((2,)), dma((width // HALF,)), dma((5,)),
            dma((2,)), dma((2,)),
            dma((2, 2, 2)), dma((2, 4)),
            dma((2,)), dma((2,)),
            dma((2, 4)), dma((2, 4)),
            dma((2,)), dma((2,)), dma((2,)),
            dma, dma, pltpu.SemaphoreType.REGULAR,
        ],
        compiler_params=pltpu.CompilerParams(
            collective_id=0, has_side_effects=True, vmem_limit_bytes=60 * 2**20
        ),
        name="ptycho",
    )(scan_offsets, specimen, probe_wave, fresnel_phase, measured, jnp.asarray(dft_tables()), jnp.asarray(order_tables()))
    return pl.pallas_call(
        functools.partial(place_kernel, width),
        out_shape=jax.ShapeDtypeStruct(specimen.shape, F32),
        in_specs=[any_space, any_space],
        out_specs=any_space,
        scratch_shapes=[
            pltpu.SMEM((3, 2, 2), jnp.int32), vm(2, 2, 6, HALF, FULL), vm(2, 2, HALF, width),
            dma, dma((2, 2)), dma((2, 2)),
        ],
        compiler_params=pltpu.CompilerParams(vmem_limit_bytes=60 * 2**20),
        name="place",
    )(near_offs, grads)


def solution(mesh):
    placed = (P("depth", None, "tile", None), P("tile", None), P(), P(), P("tile", None, None))
    return jax.shard_map(
        functools.partial(local, mesh.shape["tile"]),
        mesh=mesh, in_specs=placed, out_specs=P("depth", None, "tile", None), check_vma=False,
    )
```

```python
import functools

import jax
import jax.numpy as jnp
import ml_dtypes
import numpy as np
from jax import lax
from jax.experimental import pallas as pl
from jax.experimental.pallas import tpu as pltpu
from jax.sharding import PartitionSpec as P

MESH = pl.DeviceIdType.MESH
F32 = jnp.float32
BF16 = jnp.bfloat16
HALF = 128
FULL = 256
RING = 4
DETOURED = (1,)


def halves(matrix):
    high = matrix.astype(ml_dtypes.bfloat16)
    low = (matrix - high.astype(np.float64)).astype(ml_dtypes.bfloat16)
    return high, low


def dft_tables():
    n = np.arange(HALF)
    tables = []
    for parity in (0, 1):
        angle = 2.0 * np.pi * ((n[:, None] * (2 * n[None, :] + parity)) % FULL) / FULL
        cosine, sine = np.cos(angle) / 16.0, np.sin(angle) / 16.0
        right = np.block([[cosine, -sine], [sine, cosine]])
        tables.append(right)
    parts = [halves(m) for right in tables for m in (right, right.T)]
    return np.stack([np.stack(p) for p in parts])


def order_tables():
    order = np.concatenate([np.arange(0, FULL, 2), np.arange(1, FULL, 2)])
    right = np.zeros((FULL, FULL), np.float32)
    right[order, np.arange(FULL)] = 1.0
    return np.stack([right, right.T]).astype(ml_dtypes.bfloat16)


def dot(a, b):
    return jnp.dot(a, b, preferred_element_type=F32)


def two_parts(x):
    high = x.astype(BF16)
    low = (x - high.astype(F32)).astype(BF16)
    return high, low


def exact_right(x, ones):
    high = x.astype(BF16)
    rest = x - high.astype(F32)
    middle = rest.astype(BF16)
    low = (rest - middle.astype(F32)).astype(BF16)
    return (dot(high, ones) + dot(middle, ones)) + dot(low, ones)


def exact_left(ones, x):
    high = x.astype(BF16)
    rest = x - high.astype(F32)
    middle = rest.astype(BF16)
    low = (rest - middle.astype(F32)).astype(BF16)
    return (dot(ones, high) + dot(ones, middle)) + dot(ones, low)


def times_right(x, table):
    high, low = two_parts(x)
    return dot(high, table[0]) + (dot(low, table[0]) + dot(high, table[1]))


def times_left(table, x):
    high, low = two_parts(x)
    return dot(table[0], high) + (dot(table[0], low) + dot(table[1], high))


EVEN, EVEN_T, ODD, ODD_T = range(4)


def forward_transform(x_ref, z_ref, tab):
    re, im = x_ref[0], x_ref[1]
    even = jnp.concatenate([re[:, :HALF] + re[:, HALF:], im[:, :HALF] + im[:, HALF:]], 1)
    odd = jnp.concatenate([re[:, :HALF] - re[:, HALF:], im[:, :HALF] - im[:, HALF:]], 1)
    ye = times_right(even, tab.at[EVEN])
    yo = times_right(odd, tab.at[ODD])
    re = jnp.concatenate([ye[:, :HALF], yo[:, :HALF]], 1)
    im = jnp.concatenate([ye[:, HALF:], yo[:, HALF:]], 1)
    z_ref[0] = times_left(tab.at[EVEN_T], jnp.concatenate([re[:HALF] + re[HALF:], im[:HALF] + im[HALF:]], 0))
    z_ref[1] = times_left(tab.at[ODD_T], jnp.concatenate([re[:HALF] - re[HALF:], im[:HALF] - im[HALF:]], 0))


def inverse_transform(z_ref, out, tab):
    a = times_left(tab.at[EVEN], z_ref[0])
    b = times_left(tab.at[ODD], z_ref[1])
    total, rest = a + b, a - b
    re = jnp.concatenate([total[:HALF], rest[:HALF]], 0)
    im = jnp.concatenate([total[HALF:], rest[HALF:]], 0)
    a = times_right(jnp.concatenate([re[:, :HALF], im[:, :HALF]], 1), tab.at[EVEN_T])
    b = times_right(jnp.concatenate([re[:, HALF:], im[:, HALF:]], 1), tab.at[ODD_T])
    total, rest = a + b, a - b
    out[0] = jnp.concatenate([total[:, :HALF], rest[:, :HALF]], 1)
    out[1] = jnp.concatenate([total[:, HALF:], rest[:, HALF:]], 1)


def column_block(column, width):
    block = jnp.minimum(lax.shift_right_logical(column, 7), width // HALF - 3)
    return block, column - block * HALF


def take_window(spec, layer, component, column, width):
    block, shift = column_block(column, width)
    lane = lax.broadcasted_iota(jnp.int32, (HALF, HALF), 1)
    mixed = jnp.where(lane >= shift, spec[layer, component, block], spec[layer, component, block + 2])
    return mixed, spec[layer, component, block + 1]


def main_kernel(
    tiles, width,
    offs_hbm, spec_hbm, probe_hbm, phase_hbm, meas_hbm, tab_hbm, perm_hbm,
    grads, offs_out,
    offs, offs_table, spec, probe, phase, meas, tab, perm,
    staged, near, own_staged, own, patch, field, x_buf, z_buf, kern, update, relayed, offs_land,
    offs_sem, block_sem, load_sem, off_send, off_recv, in_send, in_recv, sib_send, sib_recv,
    out_send, out_recv, mid_send, mid_recv, mid_local, relay_send, relay_recv, relay_ready,
):
    me = lax.axis_index("tile")
    core = lax.axis_index("depth")
    other = 1 - core
    has_above = me > 0
    has_below = me < tiles - 1
    above = jnp.maximum(me - 1, 0)
    below = jnp.minimum(me + 1, tiles - 1)

    row = RING * RING
    ring_rows = tiles // row
    place = lax.rem(me, row)
    far_source = (place == row - 1) & has_below & (core == 1)
    relays = (me == 0) & (core == 1)
    middle = ring_rows - 2
    passes_on = (me == middle * row - 1) & (core == 1)
    far_target = (place == 0) & has_above & (core == 1)

    barrier = pltpu.get_barrier_semaphore()
    pl.semaphore_signal(barrier, inc=1, device_id=(other, me), device_id_type=MESH)

    @pl.when(has_above)
    def _():
        for d in (0, 1):
            pl.semaphore_signal(barrier, inc=1, device_id=(d, above), device_id_type=MESH)

    @pl.when(has_below)
    def _():
        for d in (0, 1):
            pl.semaphore_signal(barrier, inc=1, device_id=(d, below), device_id_type=MESH)

    @pl.when(relays)
    def _():
        for k in range(1, ring_rows):
            pl.semaphore_signal(barrier, inc=1, device_id=(1, k * row), device_id_type=MESH)
            if k <= middle:
                pl.semaphore_signal(barrier, inc=1, device_id=(1, k * row - 1), device_id_type=MESH)

    @pl.when(passes_on)
    def _():
        pl.semaphore_signal(barrier, inc=1, device_id=(1, (middle + 1) * row - 1), device_id_type=MESH)

    blocks = width // HALF

    def block_copy(b):
        return pltpu.make_async_copy(
            spec_hbm.at[:, :, :, pl.ds(b * HALF, HALF)], spec.at[:, :, b], block_sem.at[b]
        )

    loads = [
        pltpu.make_async_copy(tab_hbm, tab, load_sem.at[0]),
        pltpu.make_async_copy(perm_hbm, perm, load_sem.at[1]),
        pltpu.make_async_copy(probe_hbm, probe, load_sem.at[2]),
        pltpu.make_async_copy(phase_hbm, phase, load_sem.at[3]),
        pltpu.make_async_copy(meas_hbm.at[core], meas, load_sem.at[4]),
    ]
    offs_load = pltpu.make_async_copy(offs_hbm, offs, offs_sem.at[0])
    offs_store = pltpu.make_async_copy(offs_table, offs_out, offs_sem.at[1])
    offs_load.start()
    for b in range(blocks):
        block_copy(b).start()
    for copy in loads:
        copy.start()
    offs_load.wait()
    present = 1 + 2 * has_above.astype(jnp.int32) + 2 * has_below.astype(jnp.int32)
    pl.semaphore_wait(barrier, present + (far_source | far_target).astype(jnp.int32))

    def offsets_copy(side):
        return pltpu.make_async_remote_copy(
            src_ref=offs, dst_ref=offs_land.at[1 - side], send_sem=off_send.at[side], recv_sem=off_recv.at[1 - side],
            device_id=(core, above if side == 0 else below), device_id_type=MESH,
        )

    sides = ((0, has_above), (1, has_below))
    for side, there in sides:
        pl.when(there)(offsets_copy(side).start)

    @pl.when(far_target)
    def _():
        pl.semaphore_signal(relay_ready, inc=1, device_id=(1, 0), device_id_type=MESH)

    for b in range(blocks):
        block_copy(b).wait()
    for layer in (0, 1):
        for c in (0, 1):
            mixed, pure = take_window(spec, layer, c, offs[other, 1], width)
            own_staged[layer, c, :, :HALF] = mixed
            own_staged[layer, c, :, HALF:] = pure

    def sibling_copy(layer):
        return pltpu.make_async_remote_copy(
            src_ref=own_staged.at[layer], dst_ref=own.at[2 * core + layer], send_sem=sib_send.at[layer],
            recv_sem=sib_recv.at[layer], device_id=(other, me), device_id_type=MESH,
        )

    for layer in (0, 1):
        sibling_copy(layer).start()
    for layer in (0, 1):
        for c in (0, 1):
            mixed, pure = take_window(spec, layer, c, offs[core, 1], width)
            own[2 * core + layer, c, :, :HALF] = mixed
            own[2 * core + layer, c, :, HALF:] = pure

    def window_copy(position, layer, side):
        return pltpu.make_async_remote_copy(
            src_ref=staged.at[side, position, layer], dst_ref=near.at[1 - side, 2 * core + layer],
            send_sem=in_send.at[side, position, layer], recv_sem=in_recv.at[1 - side, 2 * core + layer],
            device_id=(position, above if side == 0 else below), device_id_type=MESH,
        )

    def detour_copy(layer):
        k = me // row
        return pltpu.make_async_remote_copy(
            src_ref=staged.at[1, 1, layer], dst_ref=relayed.at[k, layer], send_sem=in_send.at[1, 1, layer],
            recv_sem=relay_recv.at[k, layer], device_id=(1, jnp.where(k == middle, middle * row - 1, 0)),
            device_id_type=MESH,
        )

    def onward_copy(layer):
        return pltpu.make_async_remote_copy(
            src_ref=relayed.at[middle, layer], dst_ref=relayed.at[middle, layer], send_sem=relay_send.at[middle, layer],
            recv_sem=relay_recv.at[middle, layer], device_id=(1, 0), device_id_type=MESH,
        )

    def relay_copy(k, layer):
        return pltpu.make_async_remote_copy(
            src_ref=relayed.at[k, layer], dst_ref=near.at[0, 2 + layer], send_sem=relay_send.at[k, layer],
            recv_sem=in_recv.at[0, 2 + layer], device_id=(1, (k + 1) * row), device_id_type=MESH,
        )

    def wait_relayed(k, layer):
        pltpu.make_async_remote_copy(
            src_ref=relayed.at[k, layer], dst_ref=relayed.at[k, layer], send_sem=relay_send.at[k, layer],
            recv_sem=relay_recv.at[k, layer], device_id=(1, row), device_id_type=MESH,
        ).wait_recv()

    def wait_offsets(side):
        pltpu.make_async_remote_copy(
            src_ref=offs, dst_ref=offs_land.at[side], send_sem=off_send.at[side], recv_sem=off_recv.at[side],
            device_id=(core, above if side == 0 else below), device_id_type=MESH,
        ).wait_recv()

    def cut(side, position, layer):
        for c in (0, 1):
            mixed, pure = take_window(spec, layer, c, offs_land[side, position, 1], width)
            staged[side, position, layer, c, :, :HALF] = mixed
            staged[side, position, layer, c, :, HALF:] = pure

    def send(side, position, layer):
        cut(side, position, layer)
        window_copy(position, layer, side).start()

    def answer(side):
        wait_offsets(side)
        for position in (0, 1):
            for layer in (0, 1):
                send(side, position, layer)

    first_of_ring = lax.rem(me, RING) == 0
    usual = jnp.logical_not(far_source)
    pl.when(has_above & jnp.logical_not(first_of_ring) & usual)(functools.partial(answer, 0))
    pl.when(has_below & usual)(functools.partial(answer, 1))
    pl.when(has_above & first_of_ring & usual)(functools.partial(answer, 0))

    @pl.when(far_source)
    def _():
        wait_offsets(0)
        send(0, 0, 0)
        send(0, 0, 1)
        wait_offsets(1)
        cut(1, 1, 1)
        detour_copy(1).start()
        for side, position, layer in ((1, 0, 0), (0, 1, 0), (1, 0, 1), (0, 1, 1), (1, 1, 0)):
            send(side, position, layer)

    for side, there in sides:
        for position in (0, 1):
            first = offs_land[side, position, 0] - (me - 2 + 2 * side) * HALF
            offs_table[side, position, 0] = jnp.where(there, first, HALF * side)
            offs_table[side, position, 1] = jnp.where(there, offs_land[side, position, 1], 0)
    for position in (0, 1):
        offs_table[2, position, 0] = 0
        offs_table[2, position, 1] = offs[position, 1]
    offs_store.start()

    first = offs[core, 0] - (me - 1) * HALF
    unused, shift = column_block(offs[core, 1], width)
    for copy in loads:
        copy.wait()
    phases = exact_right(exact_left(perm[1], phase[...]), perm[0])
    kern[0] = jnp.cos(phases)
    kern[1] = jnp.sin(phases)
    meas[...] = exact_right(exact_left(perm[1], meas[...]), perm[0])
    rows = lax.broadcasted_iota(jnp.int32, (FULL, FULL), 0)
    cols = lax.broadcasted_iota(jnp.int32, (FULL, FULL), 1)
    turn = jnp.where(((cols + first) & (FULL - 1)) == rows, 1.0, 0.0).astype(BF16)
    slide = jnp.where(((rows + shift) & (FULL - 1)) == cols, 1.0, 0.0).astype(BF16)
    for c in (0, 1):
        field[0, c] = exact_right(exact_left(turn, probe[c]), slide)

    for layer in (0, 1):
        pltpu.make_async_remote_copy(
            src_ref=own_staged.at[layer], dst_ref=own.at[2 * other + layer], send_sem=sib_send.at[layer],
            recv_sem=sib_recv.at[layer], device_id=(other, me), device_id_type=MESH,
        ).wait_recv()

    half_rows = lax.broadcasted_iota(jnp.int32, (HALF, FULL), 0)

    def update_copy(s, side):
        target = s // 2
        return pltpu.make_async_remote_copy(
            src_ref=update.at[s, :, pl.ds(0, HALF)], dst_ref=grads.at[s - 2 * target, 2 * (1 - side) + core],
            send_sem=out_send.at[side, s], recv_sem=out_recv.at[s - 2 * target, 2 * (1 - side) + core],
            device_id=(target, above if side == 0 else below), device_id_type=MESH,
        )

    def middle_copy(layer):
        return pltpu.make_async_remote_copy(
            src_ref=update.at[2 * other + layer, :, pl.ds(HALF, HALF)], dst_ref=grads.at[layer, 4 + core],
            send_sem=mid_send.at[layer], recv_sem=mid_recv.at[layer], device_id=(other, me), device_id_type=MESH,
        )

    def middle_local(layer):
        return pltpu.make_async_copy(
            update.at[2 * core + layer, :, pl.ds(HALF, HALF)], grads.at[layer, 4 + core], mid_local.at[layer]
        )

    def step(i, carry):
        @pl.when(i <= 3)
        def _():
            for side, there in sides:
                @pl.when(there)
                def _(side=side):
                    pltpu.make_async_remote_copy(
                        src_ref=staged.at[side, 0, 0], dst_ref=near.at[side, i], send_sem=in_send.at[side, 0, 0],
                        recv_sem=in_recv.at[side, i], device_id=(core, above if side == 0 else below),
                        device_id_type=MESH,
                    ).wait_recv()
            top = [jnp.where(half_rows >= first, near[0, i, c], near[1, i, c]) for c in (0, 1)]
            bottom = [own[i, c] for c in (0, 1)]
            for c in (0, 1):
                patch[i, c, :HALF] = top[c]
                patch[i, c, HALF:] = bottom[c]
            for part, (pr, pi) in enumerate((top, bottom)):
                span = pl.ds(part * HALF, HALF)
                wr, wi = field[i, 0, span], field[i, 1, span]
                x_buf[0, span] = wr * pr - wi * pi
                x_buf[1, span] = wr * pi + wi * pr

        @pl.when(i > 3)
        def _():
            pr, pi = patch[7 - i, 0], patch[7 - i, 1]
            ar, ai = field[i, 0], field[i, 1]
            x_buf[0] = pr * ar + pi * ai
            x_buf[1] = pr * ai - pi * ar

        @pl.when(passes_on & (i == 0))
        def _():
            for layer in DETOURED:
                wait_relayed(middle, layer)
                onward_copy(layer).start()

        @pl.when(relays & (i == 1))
        def _():
            pl.semaphore_wait(relay_ready, ring_rows - 1)
            for k in range(ring_rows - 1):
                for layer in DETOURED:
                    wait_relayed(k, layer)
                    relay_copy(k, layer).start()

        forward_transform(x_buf, z_buf, tab)

        @pl.when(i == 3)
        def _():
            for parity in (0, 1):
                zr, zi = z_buf[parity, :HALF], z_buf[parity, HALF:]
                e = 2.0 * (zr * zr + zi * zi - meas[parity * HALF : (parity + 1) * HALF])
                z_buf[parity, :HALF] = e * zr
                z_buf[parity, HALF:] = e * zi

        @pl.when(i != 3)
        def _():
            sign = jnp.where(i < 3, 1.0, -1.0)
            for parity in (0, 1):
                span = slice(parity * HALF, (parity + 1) * HALF)
                zr, zi = z_buf[parity, :HALF], z_buf[parity, HALF:]
                kr, ki = kern[0, span], sign * kern[1, span]
                z_buf[parity, :HALF] = kr * zr - ki * zi
                z_buf[parity, HALF:] = kr * zi + ki * zr

        inverse_transform(z_buf, field.at[i + 1], tab)

        @pl.when(i >= 3)
        def _():
            s = 6 - i
            wr, wi = field[s, 0], field[s, 1]
            ar, ai = field[i + 1, 0], field[i + 1, 1]
            update[s, 0] = wr * ar + wi * ai
            update[s, 1] = wr * ai - wi * ar
            for side, there in sides:
                @pl.when(there)
                def _(side=side):
                    update_copy(s, side).start()
            for layer in (0, 1):
                pl.when(s == 2 * other + layer)(middle_copy(layer).start)
                pl.when(s == 2 * core + layer)(middle_local(layer).start)

        return carry

    lax.fori_loop(0, 7, step, 0)

    offs_store.wait()
    for k in range(ring_rows - 1):
        for layer in DETOURED:
            pl.when(relays)(relay_copy(k, layer).wait_send)
    for layer in DETOURED:
        pl.when(passes_on)(onward_copy(layer).wait_send)
    for layer in (0, 1):
        middle_local(layer).wait()
        middle_copy(layer).wait_send()
        pltpu.make_async_remote_copy(
            src_ref=update.at[0, :, pl.ds(HALF, HALF)], dst_ref=grads.at[layer, 4 + other],
            send_sem=mid_send.at[layer], recv_sem=mid_recv.at[layer], device_id=(other, me), device_id_type=MESH,
        ).wait_recv()
        sibling_copy(layer).wait_send()
    for side, there in sides:
        @pl.when(there)
        def _(side=side):
            offsets_copy(side).wait_send()
            for position in (0, 1):
                for layer in (0, 1):
                    window_copy(position, layer, side).wait_send()
            for s in range(4):
                update_copy(s, side).wait_send()
            for layer in (0, 1):
                for position in (0, 1):
                    pltpu.make_async_remote_copy(
                        src_ref=update.at[0, :, pl.ds(0, HALF)], dst_ref=grads.at[layer, 2 * side + position],
                        send_sem=out_send.at[side, 0], recv_sem=out_recv.at[layer, 2 * side + position],
                        device_id=(core, above if side == 0 else below), device_id_type=MESH,
                    ).wait_recv()


def place_kernel(width, offs_hbm, grads, out, offs, held, strip, offs_sem, in_sem, out_sem):
    def in_copy(layer, c):
        return pltpu.make_async_copy(grads.at[layer, :, c], held.at[layer, c], in_sem.at[layer, c])

    def out_copy(layer, c):
        return pltpu.make_async_copy(strip.at[layer, c], out.at[layer, c], out_sem.at[layer, c])

    parts = [(layer, c) for layer in (0, 1) for c in (0, 1)]
    offs_load = pltpu.make_async_copy(offs_hbm, offs, offs_sem)
    offs_load.start()
    for part in parts:
        in_copy(*part).start()
    strip[...] = jnp.zeros_like(strip)
    row = lax.broadcasted_iota(jnp.int32, (HALF, FULL), 0)
    lane = lax.broadcasted_iota(jnp.int32, (HALF, HALF), 1)
    offs_load.wait()
    for layer, c in parts:
        in_copy(layer, c).wait()
        for window in range(6):
            side, position = window // 2, window % 2
            block, shift = column_block(offs[side, position, 1], width)
            value = held[layer, c, window]
            if side == 0:
                value = jnp.where(row < offs[0, position, 0], value, 0.0)
            elif side == 1:
                value = jnp.where(row >= offs[1, position, 0], value, 0.0)
            mixed, pure = value[:, :HALF], value[:, HALF:]
            first = lane >= shift
            for k, piece in enumerate((jnp.where(first, mixed, 0.0), pure, jnp.where(first, 0.0, mixed))):
                span = pl.ds(pl.multiple_of((block + k) * HALF, HALF), HALF)
                strip[layer, c, :, span] += piece
        out_copy(layer, c).start()
    for part in parts:
        out_copy(*part).wait()


def local(tiles, specimen, scan_offsets, probe_wave, fresnel_phase, measured):
    width = specimen.shape[3]
    any_space = pl.BlockSpec(memory_space=pl.ANY)
    dma = pltpu.SemaphoreType.DMA
    vm = lambda *shape: pltpu.VMEM(shape, F32)
    grads, near_offs = pl.pallas_call(
        functools.partial(main_kernel, tiles, width),
        out_shape=[
            jax.ShapeDtypeStruct((2, 6, 2, HALF, FULL), F32),
            jax.ShapeDtypeStruct((3, 2, 2), jnp.int32),
        ],
        in_specs=[any_space] * 7,
        out_specs=[any_space, any_space],
        scratch_shapes=[
            pltpu.SMEM((2, 2), jnp.int32),
            pltpu.SMEM((3, 2, 2), jnp.int32),
            vm(2, 2, width // HALF, HALF, HALF),
            vm(2, FULL, FULL),
            vm(FULL, FULL),
            vm(FULL, FULL),
            pltpu.VMEM((4, 2, FULL, FULL), BF16),
            pltpu.VMEM((2, FULL, FULL), BF16),
            vm(2, 2, 2, 2, HALF, FULL),
            vm(2, 4, 2, HALF, FULL),
            vm(2, 2, HALF, FULL),
            vm(4, 2, HALF, FULL),
            vm(4, 2, FULL, FULL),
            vm(8, 2, FULL, FULL),
            vm(2, FULL, FULL),
            vm(2, FULL, FULL),
            vm(2, FULL, FULL),
            vm(4, 2, FULL, FULL),
            vm(tiles // (RING * RING) - 1, 2, 2, HALF, FULL),
            pltpu.SMEM((2, 2, 2), jnp.int32),
            dma((2,)), dma((width // HALF,)), dma((5,)),
            dma((2,)), dma((2,)),
            dma((2, 2, 2)), dma((2, 4)),
            dma((2,)), dma((2,)),
            dma((2, 4)), dma((2, 4)),
            dma((2,)), dma((2,)), dma((2,)),
            dma((tiles // (RING * RING) - 1, 2)), dma((tiles // (RING * RING) - 1, 2)), pltpu.SemaphoreType.REGULAR,
        ],
        compiler_params=pltpu.CompilerParams(
            collective_id=0, has_side_effects=True, vmem_limit_bytes=60 * 2**20
        ),
        name="ptycho",
    )(scan_offsets, specimen, probe_wave, fresnel_phase, measured, jnp.asarray(dft_tables()), jnp.asarray(order_tables()))
    return pl.pallas_call(
        functools.partial(place_kernel, width),
        out_shape=jax.ShapeDtypeStruct(specimen.shape, F32),
        in_specs=[any_space, any_space],
        out_specs=any_space,
        scratch_shapes=[
            pltpu.SMEM((3, 2, 2), jnp.int32), vm(2, 2, 6, HALF, FULL), vm(2, 2, HALF, width),
            dma, dma((2, 2)), dma((2, 2)),
        ],
        compiler_params=pltpu.CompilerParams(vmem_limit_bytes=60 * 2**20),
        name="place",
    )(near_offs, grads)


def solution(mesh):
    placed = (P("depth", None, "tile", None), P("tile", None), P(), P(), P("tile", None, None))
    return jax.shard_map(
        functools.partial(local, mesh.shape["tile"]),
        mesh=mesh, in_specs=placed, out_specs=P("depth", None, "tile", None), check_vma=False,
    )
```

```python
import functools

import jax
import jax.numpy as jnp
import ml_dtypes
import numpy as np
from jax import lax
from jax.experimental import pallas as pl
from jax.experimental.pallas import tpu as pltpu
from jax.sharding import PartitionSpec as P

MESH = pl.DeviceIdType.MESH
F32 = jnp.float32
BF16 = jnp.bfloat16
HALF = 128
FULL = 256
RING = 4
DETOURED = (1,)


def halves(matrix):
    high = matrix.astype(ml_dtypes.bfloat16)
    low = (matrix - high.astype(np.float64)).astype(ml_dtypes.bfloat16)
    return high, low


def dft_tables():
    n = np.arange(HALF)
    tables = []
    for parity in (0, 1):
        angle = 2.0 * np.pi * ((n[:, None] * (2 * n[None, :] + parity)) % FULL) / FULL
        cosine, sine = np.cos(angle) / 16.0, np.sin(angle) / 16.0
        right = np.block([[cosine, -sine], [sine, cosine]])
        tables.append(right)
    parts = [halves(m) for right in tables for m in (right, right.T)]
    return np.stack([np.stack(p) for p in parts])


def order_tables():
    order = np.concatenate([np.arange(0, FULL, 2), np.arange(1, FULL, 2)])
    right = np.zeros((FULL, FULL), np.float32)
    right[order, np.arange(FULL)] = 1.0
    return np.stack([right, right.T]).astype(ml_dtypes.bfloat16)


def dot(a, b):
    return jnp.dot(a, b, preferred_element_type=F32)


def two_parts(x):
    high = x.astype(BF16)
    low = (x - high.astype(F32)).astype(BF16)
    return high, low


def exact_right(x, ones):
    high = x.astype(BF16)
    rest = x - high.astype(F32)
    middle = rest.astype(BF16)
    low = (rest - middle.astype(F32)).astype(BF16)
    return (dot(high, ones) + dot(middle, ones)) + dot(low, ones)


def exact_left(ones, x):
    high = x.astype(BF16)
    rest = x - high.astype(F32)
    middle = rest.astype(BF16)
    low = (rest - middle.astype(F32)).astype(BF16)
    return (dot(ones, high) + dot(ones, middle)) + dot(ones, low)


def times_right(x, table):
    high, low = two_parts(x)
    return dot(high, table[0]) + (dot(low, table[0]) + dot(high, table[1]))


def times_left(table, x):
    high, low = two_parts(x)
    return dot(table[0], high) + (dot(table[0], low) + dot(table[1], high))


EVEN, EVEN_T, ODD, ODD_T = range(4)


def forward_transform(x_ref, z_ref, tab):
    re, im = x_ref[0], x_ref[1]
    even = jnp.concatenate([re[:, :HALF] + re[:, HALF:], im[:, :HALF] + im[:, HALF:]], 1)
    odd = jnp.concatenate([re[:, :HALF] - re[:, HALF:], im[:, :HALF] - im[:, HALF:]], 1)
    ye = times_right(even, tab.at[EVEN])
    yo = times_right(odd, tab.at[ODD])
    re = jnp.concatenate([ye[:, :HALF], yo[:, :HALF]], 1)
    im = jnp.concatenate([ye[:, HALF:], yo[:, HALF:]], 1)
    z_ref[0] = times_left(tab.at[EVEN_T], jnp.concatenate([re[:HALF] + re[HALF:], im[:HALF] + im[HALF:]], 0))
    z_ref[1] = times_left(tab.at[ODD_T], jnp.concatenate([re[:HALF] - re[HALF:], im[:HALF] - im[HALF:]], 0))


def inverse_transform(z_ref, out, tab):
    a = times_left(tab.at[EVEN], z_ref[0])
    b = times_left(tab.at[ODD], z_ref[1])
    total, rest = a + b, a - b
    re = jnp.concatenate([total[:HALF], rest[:HALF]], 0)
    im = jnp.concatenate([total[HALF:], rest[HALF:]], 0)
    a = times_right(jnp.concatenate([re[:, :HALF], im[:, :HALF]], 1), tab.at[EVEN_T])
    b = times_right(jnp.concatenate([re[:, HALF:], im[:, HALF:]], 1), tab.at[ODD_T])
    total, rest = a + b, a - b
    out[0] = jnp.concatenate([total[:, :HALF], rest[:, :HALF]], 1)
    out[1] = jnp.concatenate([total[:, HALF:], rest[:, HALF:]], 1)


def column_block(column, width):
    block = jnp.minimum(lax.shift_right_logical(column, 7), width // HALF - 3)
    return block, column - block * HALF


def take_window(spec, layer, component, column, width):
    block, shift = column_block(column, width)
    lane = lax.broadcasted_iota(jnp.int32, (HALF, HALF), 1)
    mixed = jnp.where(lane >= shift, spec[layer, component, block], spec[layer, component, block + 2])
    return mixed, spec[layer, component, block + 1]


def main_kernel(
    tiles, width,
    offs_hbm, spec_hbm, probe_hbm, phase_hbm, meas_hbm, tab_hbm, perm_hbm,
    grads, offs_out,
    offs, offs_table, spec, probe, phase, meas, tab, perm,
    staged, near, own_staged, own, patch, field, x_buf, z_buf, kern, update, relayed, offs_land,
    offs_sem, block_sem, load_sem, off_send, off_recv, in_send, in_recv, sib_send, sib_recv,
    out_send, out_recv, mid_send, mid_recv, mid_local, relay_send, relay_recv, relay_ready,
):
    me = lax.axis_index("tile")
    core = lax.axis_index("depth")
    other = 1 - core
    has_above = me > 0
    has_below = me < tiles - 1
    above = jnp.maximum(me - 1, 0)
    below = jnp.minimum(me + 1, tiles - 1)

    row = RING * RING
    ring_rows = tiles // row
    place = lax.rem(me, row)
    far_source = (place == row - 1) & has_below & (core == 1)
    relays = (me == 0) & (core == 1)
    middle = ring_rows - 2
    passes_on = (me == middle * row - 1) & (core == 1)
    far_target = (place == 0) & has_above & (core == 1)

    barrier = pltpu.get_barrier_semaphore()
    pl.semaphore_signal(barrier, inc=1, device_id=(other, me), device_id_type=MESH)

    @pl.when(has_above)
    def _():
        for d in (0, 1):
            pl.semaphore_signal(barrier, inc=1, device_id=(d, above), device_id_type=MESH)

    row_starts = (place == 0) & has_above
    row_ends = (place == row - 1) & has_below
    early = row_starts & (core == 0)

    @pl.when(has_below)
    def _():
        pl.semaphore_signal(barrier, inc=1, device_id=(1, below), device_id_type=MESH)

    @pl.when(has_below & jnp.logical_not(row_ends))
    def _():
        pl.semaphore_signal(barrier, inc=1, device_id=(0, below), device_id_type=MESH)

    @pl.when(relays)
    def _():
        for k in range(1, ring_rows):
            pl.semaphore_signal(barrier, inc=1, device_id=(1, k * row), device_id_type=MESH)
            if k <= middle:
                pl.semaphore_signal(barrier, inc=1, device_id=(1, k * row - 1), device_id_type=MESH)

    @pl.when(passes_on)
    def _():
        pl.semaphore_signal(barrier, inc=1, device_id=(1, (middle + 1) * row - 1), device_id_type=MESH)

    blocks = width // HALF

    def block_copy(b):
        return pltpu.make_async_copy(
            spec_hbm.at[:, :, :, pl.ds(b * HALF, HALF)], spec.at[:, :, b], block_sem.at[b]
        )

    loads = [
        pltpu.make_async_copy(tab_hbm, tab, load_sem.at[0]),
        pltpu.make_async_copy(perm_hbm, perm, load_sem.at[1]),
        pltpu.make_async_copy(probe_hbm, probe, load_sem.at[2]),
        pltpu.make_async_copy(phase_hbm, phase, load_sem.at[3]),
        pltpu.make_async_copy(meas_hbm.at[core], meas, load_sem.at[4]),
    ]
    offs_load = pltpu.make_async_copy(offs_hbm, offs, offs_sem.at[0])
    offs_store = pltpu.make_async_copy(offs_table, offs_out, offs_sem.at[1])
    offs_load.start()
    for b in range(blocks):
        block_copy(b).start()
    for copy in loads:
        copy.start()
    offs_load.wait()
    present = 1 + 2 * has_above.astype(jnp.int32) + 2 * has_below.astype(jnp.int32)
    present += (far_source | far_target).astype(jnp.int32) - 2 * early.astype(jnp.int32)
    pl.semaphore_wait(barrier, present)

    def offsets_copy(side):
        return pltpu.make_async_remote_copy(
            src_ref=offs, dst_ref=offs_land.at[1 - side], send_sem=off_send.at[side], recv_sem=off_recv.at[1 - side],
            device_id=(core, above if side == 0 else below), device_id_type=MESH,
        )

    sides = ((0, has_above), (1, has_below))
    def offsets_across():
        return pltpu.make_async_remote_copy(
            src_ref=offs, dst_ref=offs_land.at[1], send_sem=off_send.at[2], recv_sem=off_recv.at[1],
            device_id=(0, above), device_id_type=MESH,
        )

    pl.when(has_above & jnp.logical_not(early))(offsets_copy(0).start)
    pl.when(has_below)(offsets_copy(1).start)
    pl.when(row_starts & (core == 1))(offsets_across().start)

    @pl.when(far_target)
    def _():
        pl.semaphore_signal(relay_ready, inc=1, device_id=(1, 0), device_id_type=MESH)

    for b in range(blocks):
        block_copy(b).wait()
    for layer in (0, 1):
        for c in (0, 1):
            mixed, pure = take_window(spec, layer, c, offs[other, 1], width)
            own_staged[layer, c, :, :HALF] = mixed
            own_staged[layer, c, :, HALF:] = pure

    def sibling_copy(layer):
        return pltpu.make_async_remote_copy(
            src_ref=own_staged.at[layer], dst_ref=own.at[2 * core + layer], send_sem=sib_send.at[layer],
            recv_sem=sib_recv.at[layer], device_id=(other, me), device_id_type=MESH,
        )

    for layer in (0, 1):
        sibling_copy(layer).start()
    for layer in (0, 1):
        for c in (0, 1):
            mixed, pure = take_window(spec, layer, c, offs[core, 1], width)
            own[2 * core + layer, c, :, :HALF] = mixed
            own[2 * core + layer, c, :, HALF:] = pure

    def window_copy(position, layer, side):
        return pltpu.make_async_remote_copy(
            src_ref=staged.at[side, position, layer], dst_ref=near.at[1 - side, 2 * core + layer],
            send_sem=in_send.at[side, position, layer], recv_sem=in_recv.at[1 - side, 2 * core + layer],
            device_id=(position, above if side == 0 else below), device_id_type=MESH,
        )

    def detour_copy(layer):
        k = me // row
        return pltpu.make_async_remote_copy(
            src_ref=staged.at[1, 1, layer], dst_ref=relayed.at[k, layer], send_sem=in_send.at[1, 1, layer],
            recv_sem=relay_recv.at[k, layer], device_id=(1, jnp.where(k == middle, middle * row - 1, 0)),
            device_id_type=MESH,
        )

    def onward_copy(layer):
        return pltpu.make_async_remote_copy(
            src_ref=relayed.at[middle, layer], dst_ref=relayed.at[middle, layer], send_sem=relay_send.at[middle, layer],
            recv_sem=relay_recv.at[middle, layer], device_id=(1, 0), device_id_type=MESH,
        )

    def relay_copy(k, layer):
        return pltpu.make_async_remote_copy(
            src_ref=relayed.at[k, layer], dst_ref=near.at[0, 2 + layer], send_sem=relay_send.at[k, layer],
            recv_sem=in_recv.at[0, 2 + layer], device_id=(1, (k + 1) * row), device_id_type=MESH,
        )

    def wait_relayed(k, layer):
        pltpu.make_async_remote_copy(
            src_ref=relayed.at[k, layer], dst_ref=relayed.at[k, layer], send_sem=relay_send.at[k, layer],
            recv_sem=relay_recv.at[k, layer], device_id=(1, row), device_id_type=MESH,
        ).wait_recv()

    def wait_offsets(side):
        pltpu.make_async_remote_copy(
            src_ref=offs, dst_ref=offs_land.at[side], send_sem=off_send.at[side], recv_sem=off_recv.at[side],
            device_id=(core, above if side == 0 else below), device_id_type=MESH,
        ).wait_recv()

    def cut(side, position, layer):
        for c in (0, 1):
            mixed, pure = take_window(spec, layer, c, offs_land[side, position, 1], width)
            staged[side, position, layer, c, :, :HALF] = mixed
            staged[side, position, layer, c, :, HALF:] = pure

    def send(side, position, layer):
        cut(side, position, layer)
        window_copy(position, layer, side).start()

    def answer(near_side):
        far_side = 1 - near_side
        for position in (0, 1):
            for side in (near_side, far_side):
                @pl.when(sides[side][1])
                def _(position=position, side=side):
                    if position == 0:
                        wait_offsets(side)
                    for layer in (0, 1):
                        if near_side == 0 and side == 1 and position == 1 and layer == 1:
                            cut(side, position, layer)
                            pl.when(far_source)(detour_copy(layer).start)
                            pl.when(jnp.logical_not(far_source))(window_copy(position, layer, side).start)
                        else:
                            send(side, position, layer)

    first_of_ring = lax.rem(me, RING) == 0
    pl.when(first_of_ring)(functools.partial(answer, 1))
    pl.when(jnp.logical_not(first_of_ring))(functools.partial(answer, 0))

    for side, there in sides:
        for position in (0, 1):
            first = offs_land[side, position, 0] - (me - 2 + 2 * side) * HALF
            offs_table[side, position, 0] = jnp.where(there, first, HALF * side)
            offs_table[side, position, 1] = jnp.where(there, offs_land[side, position, 1], 0)
    for position in (0, 1):
        offs_table[2, position, 0] = 0
        offs_table[2, position, 1] = offs[position, 1]
    offs_store.start()

    first = offs[core, 0] - (me - 1) * HALF
    unused, shift = column_block(offs[core, 1], width)
    for copy in loads:
        copy.wait()
    phases = exact_right(exact_left(perm[1], phase[...]), perm[0])
    kern[0] = jnp.cos(phases)
    kern[1] = jnp.sin(phases)
    meas[...] = exact_right(exact_left(perm[1], meas[...]), perm[0])
    rows = lax.broadcasted_iota(jnp.int32, (FULL, FULL), 0)
    cols = lax.broadcasted_iota(jnp.int32, (FULL, FULL), 1)
    turn = jnp.where(((cols + first) & (FULL - 1)) == rows, 1.0, 0.0).astype(BF16)
    slide = jnp.where(((rows + shift) & (FULL - 1)) == cols, 1.0, 0.0).astype(BF16)
    for c in (0, 1):
        field[0, c] = exact_right(exact_left(turn, probe[c]), slide)

    for layer in (0, 1):
        pltpu.make_async_remote_copy(
            src_ref=own_staged.at[layer], dst_ref=own.at[2 * other + layer], send_sem=sib_send.at[layer],
            recv_sem=sib_recv.at[layer], device_id=(other, me), device_id_type=MESH,
        ).wait_recv()

    half_rows = lax.broadcasted_iota(jnp.int32, (HALF, FULL), 0)

    def update_copy(s, side):
        target = s // 2
        return pltpu.make_async_remote_copy(
            src_ref=update.at[s, :, pl.ds(0, HALF)], dst_ref=grads.at[s - 2 * target, 2 * (1 - side) + core],
            send_sem=out_send.at[side, s], recv_sem=out_recv.at[s - 2 * target, 2 * (1 - side) + core],
            device_id=(target, above if side == 0 else below), device_id_type=MESH,
        )

    def middle_copy(layer):
        return pltpu.make_async_remote_copy(
            src_ref=update.at[2 * other + layer, :, pl.ds(HALF, HALF)], dst_ref=grads.at[layer, 4 + core],
            send_sem=mid_send.at[layer], recv_sem=mid_recv.at[layer], device_id=(other, me), device_id_type=MESH,
        )

    def middle_local(layer):
        return pltpu.make_async_copy(
            update.at[2 * core + layer, :, pl.ds(HALF, HALF)], grads.at[layer, 4 + core], mid_local.at[layer]
        )

    def step(i, carry):
        @pl.when(i <= 3)
        def _():
            for side, there in sides:
                @pl.when(there)
                def _(side=side):
                    pltpu.make_async_remote_copy(
                        src_ref=staged.at[side, 0, 0], dst_ref=near.at[side, i], send_sem=in_send.at[side, 0, 0],
                        recv_sem=in_recv.at[side, i], device_id=(core, above if side == 0 else below),
                        device_id_type=MESH,
                    ).wait_recv()
            top = [jnp.where(half_rows >= first, near[0, i, c], near[1, i, c]) for c in (0, 1)]
            bottom = [own[i, c] for c in (0, 1)]
            for c in (0, 1):
                patch[i, c, :HALF] = top[c]
                patch[i, c, HALF:] = bottom[c]
            for part, (pr, pi) in enumerate((top, bottom)):
                span = pl.ds(part * HALF, HALF)
                wr, wi = field[i, 0, span], field[i, 1, span]
                x_buf[0, span] = wr * pr - wi * pi
                x_buf[1, span] = wr * pi + wi * pr

        @pl.when(i > 3)
        def _():
            pr, pi = patch[7 - i, 0], patch[7 - i, 1]
            ar, ai = field[i, 0], field[i, 1]
            x_buf[0] = pr * ar + pi * ai
            x_buf[1] = pr * ai - pi * ar

        @pl.when(passes_on & (i == 0))
        def _():
            for layer in DETOURED:
                wait_relayed(middle, layer)
                onward_copy(layer).start()

        @pl.when(relays & (i == 1))
        def _():
            pl.semaphore_wait(relay_ready, ring_rows - 1)
            for k in range(ring_rows - 1):
                for layer in DETOURED:
                    wait_relayed(k, layer)
                    relay_copy(k, layer).start()

        forward_transform(x_buf, z_buf, tab)

        @pl.when(i == 3)
        def _():
            for parity in (0, 1):
                zr, zi = z_buf[parity, :HALF], z_buf[parity, HALF:]
                e = 2.0 * (zr * zr + zi * zi - meas[parity * HALF : (parity + 1) * HALF])
                z_buf[parity, :HALF] = e * zr
                z_buf[parity, HALF:] = e * zi

        @pl.when(i != 3)
        def _():
            sign = jnp.where(i < 3, 1.0, -1.0)
            for parity in (0, 1):
                span = slice(parity * HALF, (parity + 1) * HALF)
                zr, zi = z_buf[parity, :HALF], z_buf[parity, HALF:]
                kr, ki = kern[0, span], sign * kern[1, span]
                z_buf[parity, :HALF] = kr * zr - ki * zi
                z_buf[parity, HALF:] = kr * zi + ki * zr

        inverse_transform(z_buf, field.at[i + 1], tab)

        @pl.when(i >= 3)
        def _():
            s = 6 - i
            wr, wi = field[s, 0], field[s, 1]
            ar, ai = field[i + 1, 0], field[i + 1, 1]
            update[s, 0] = wr * ar + wi * ai
            update[s, 1] = wr * ai - wi * ar
            for side, there in sides:
                @pl.when(there)
                def _(side=side):
                    update_copy(s, side).start()
            for layer in (0, 1):
                pl.when(s == 2 * other + layer)(middle_copy(layer).start)
                pl.when(s == 2 * core + layer)(middle_local(layer).start)

        return carry

    lax.fori_loop(0, 7, step, 0)

    offs_store.wait()
    for k in range(ring_rows - 1):
        for layer in DETOURED:
            pl.when(relays)(relay_copy(k, layer).wait_send)
    for layer in DETOURED:
        pl.when(passes_on)(onward_copy(layer).wait_send)
    pl.when(has_above & jnp.logical_not(early))(offsets_copy(0).wait_send)
    pl.when(has_below)(offsets_copy(1).wait_send)
    pl.when(row_starts & (core == 1))(offsets_across().wait_send)
    for layer in (0, 1):
        middle_local(layer).wait()
        middle_copy(layer).wait_send()
        pltpu.make_async_remote_copy(
            src_ref=update.at[0, :, pl.ds(HALF, HALF)], dst_ref=grads.at[layer, 4 + other],
            send_sem=mid_send.at[layer], recv_sem=mid_recv.at[layer], device_id=(other, me), device_id_type=MESH,
        ).wait_recv()
        sibling_copy(layer).wait_send()
    for side, there in sides:
        @pl.when(there)
        def _(side=side):
            for position in (0, 1):
                for layer in (0, 1):
                    window_copy(position, layer, side).wait_send()
            for s in range(4):
                update_copy(s, side).wait_send()
            for layer in (0, 1):
                for position in (0, 1):
                    pltpu.make_async_remote_copy(
                        src_ref=update.at[0, :, pl.ds(0, HALF)], dst_ref=grads.at[layer, 2 * side + position],
                        send_sem=out_send.at[side, 0], recv_sem=out_recv.at[layer, 2 * side + position],
                        device_id=(core, above if side == 0 else below), device_id_type=MESH,
                    ).wait_recv()


def place_kernel(width, offs_hbm, grads, out, offs, held, strip, offs_sem, in_sem, out_sem):
    def in_copy(layer, c):
        return pltpu.make_async_copy(grads.at[layer, :, c], held.at[layer, c], in_sem.at[layer, c])

    def out_copy(layer, c):
        return pltpu.make_async_copy(strip.at[layer, c], out.at[layer, c], out_sem.at[layer, c])

    parts = [(layer, c) for layer in (0, 1) for c in (0, 1)]
    offs_load = pltpu.make_async_copy(offs_hbm, offs, offs_sem)
    offs_load.start()
    for part in parts:
        in_copy(*part).start()
    strip[...] = jnp.zeros_like(strip)
    row = lax.broadcasted_iota(jnp.int32, (HALF, FULL), 0)
    lane = lax.broadcasted_iota(jnp.int32, (HALF, HALF), 1)
    offs_load.wait()
    for layer, c in parts:
        in_copy(layer, c).wait()
        for window in range(6):
            side, position = window // 2, window % 2
            block, shift = column_block(offs[side, position, 1], width)
            value = held[layer, c, window]
            if side == 0:
                value = jnp.where(row < offs[0, position, 0], value, 0.0)
            elif side == 1:
                value = jnp.where(row >= offs[1, position, 0], value, 0.0)
            mixed, pure = value[:, :HALF], value[:, HALF:]
            first = lane >= shift
            for k, piece in enumerate((jnp.where(first, mixed, 0.0), pure, jnp.where(first, 0.0, mixed))):
                span = pl.ds(pl.multiple_of((block + k) * HALF, HALF), HALF)
                strip[layer, c, :, span] += piece
        out_copy(layer, c).start()
    for part in parts:
        out_copy(*part).wait()


def local(tiles, specimen, scan_offsets, probe_wave, fresnel_phase, measured):
    width = specimen.shape[3]
    any_space = pl.BlockSpec(memory_space=pl.ANY)
    dma = pltpu.SemaphoreType.DMA
    vm = lambda *shape: pltpu.VMEM(shape, F32)
    grads, near_offs = pl.pallas_call(
        functools.partial(main_kernel, tiles, width),
        out_shape=[
            jax.ShapeDtypeStruct((2, 6, 2, HALF, FULL), F32),
            jax.ShapeDtypeStruct((3, 2, 2), jnp.int32),
        ],
        in_specs=[any_space] * 7,
        out_specs=[any_space, any_space],
        scratch_shapes=[
            pltpu.SMEM((2, 2), jnp.int32),
            pltpu.SMEM((3, 2, 2), jnp.int32),
            vm(2, 2, width // HALF, HALF, HALF),
            vm(2, FULL, FULL),
            vm(FULL, FULL),
            vm(FULL, FULL),
            pltpu.VMEM((4, 2, FULL, FULL), BF16),
            pltpu.VMEM((2, FULL, FULL), BF16),
            vm(2, 2, 2, 2, HALF, FULL),
            vm(2, 4, 2, HALF, FULL),
            vm(2, 2, HALF, FULL),
            vm(4, 2, HALF, FULL),
            vm(4, 2, FULL, FULL),
            vm(8, 2, FULL, FULL),
            vm(2, FULL, FULL),
            vm(2, FULL, FULL),
            vm(2, FULL, FULL),
            vm(4, 2, FULL, FULL),
            vm(tiles // (RING * RING) - 1, 2, 2, HALF, FULL),
            pltpu.SMEM((2, 2, 2), jnp.int32),
            dma((2,)), dma((width // HALF,)), dma((5,)),
            dma((3,)), dma((2,)),
            dma((2, 2, 2)), dma((2, 4)),
            dma((2,)), dma((2,)),
            dma((2, 4)), dma((2, 4)),
            dma((2,)), dma((2,)), dma((2,)),
            dma((tiles // (RING * RING) - 1, 2)), dma((tiles // (RING * RING) - 1, 2)), pltpu.SemaphoreType.REGULAR,
        ],
        compiler_params=pltpu.CompilerParams(
            collective_id=0, has_side_effects=True, vmem_limit_bytes=60 * 2**20
        ),
        name="ptycho",
    )(scan_offsets, specimen, probe_wave, fresnel_phase, measured, jnp.asarray(dft_tables()), jnp.asarray(order_tables()))
    return pl.pallas_call(
        functools.partial(place_kernel, width),
        out_shape=jax.ShapeDtypeStruct(specimen.shape, F32),
        in_specs=[any_space, any_space],
        out_specs=any_space,
        scratch_shapes=[
            pltpu.SMEM((3, 2, 2), jnp.int32), vm(2, 2, 6, HALF, FULL), vm(2, 2, HALF, width),
            dma, dma((2, 2)), dma((2, 2)),
        ],
        compiler_params=pltpu.CompilerParams(vmem_limit_bytes=60 * 2**20),
        name="place",
    )(near_offs, grads)


def solution(mesh):
    placed = (P("depth", None, "tile", None), P("tile", None), P(), P(), P("tile", None, None))
    return jax.shard_map(
        functools.partial(local, mesh.shape["tile"]),
        mesh=mesh, in_specs=placed, out_specs=P("depth", None, "tile", None), check_vma=False,
    )
```

```python
import functools

import jax
import jax.numpy as jnp
import ml_dtypes
import numpy as np
from jax import lax
from jax.experimental import pallas as pl
from jax.experimental.pallas import tpu as pltpu
from jax.sharding import PartitionSpec as P

MESH = pl.DeviceIdType.MESH
F32 = jnp.float32
BF16 = jnp.bfloat16
HALF = 128
FULL = 256
RING = 4
DETOURED = (1,)


def halves(matrix):
    high = matrix.astype(ml_dtypes.bfloat16)
    low = (matrix - high.astype(np.float64)).astype(ml_dtypes.bfloat16)
    return high, low


def dft_tables():
    n = np.arange(HALF)
    tables = []
    for parity in (0, 1):
        angle = 2.0 * np.pi * ((n[:, None] * (2 * n[None, :] + parity)) % FULL) / FULL
        cosine, sine = np.cos(angle) / 16.0, np.sin(angle) / 16.0
        right = np.block([[cosine, -sine], [sine, cosine]])
        tables.append(right)
    parts = [halves(m) for right in tables for m in (right, right.T)]
    return np.stack([np.stack(p) for p in parts])


def order_tables():
    order = np.concatenate([np.arange(0, FULL, 2), np.arange(1, FULL, 2)])
    right = np.zeros((FULL, FULL), np.float32)
    right[order, np.arange(FULL)] = 1.0
    return np.stack([right, right.T]).astype(ml_dtypes.bfloat16)


def dot(a, b):
    return jnp.dot(a, b, preferred_element_type=F32)


def two_parts(x):
    high = x.astype(BF16)
    low = (x - high.astype(F32)).astype(BF16)
    return high, low


def exact_right(x, ones):
    high = x.astype(BF16)
    rest = x - high.astype(F32)
    middle = rest.astype(BF16)
    low = (rest - middle.astype(F32)).astype(BF16)
    return (dot(high, ones) + dot(middle, ones)) + dot(low, ones)


def exact_left(ones, x):
    high = x.astype(BF16)
    rest = x - high.astype(F32)
    middle = rest.astype(BF16)
    low = (rest - middle.astype(F32)).astype(BF16)
    return (dot(ones, high) + dot(ones, middle)) + dot(ones, low)


def times_right(x, table):
    high, low = two_parts(x)
    return dot(high, table[0]) + (dot(low, table[0]) + dot(high, table[1]))


def times_left(table, x):
    high, low = two_parts(x)
    return dot(table[0], high) + (dot(table[0], low) + dot(table[1], high))


EVEN, EVEN_T, ODD, ODD_T = range(4)


def forward_transform(x_ref, z_ref, tab):
    re, im = x_ref[0], x_ref[1]
    even = jnp.concatenate([re[:, :HALF] + re[:, HALF:], im[:, :HALF] + im[:, HALF:]], 1)
    odd = jnp.concatenate([re[:, :HALF] - re[:, HALF:], im[:, :HALF] - im[:, HALF:]], 1)
    ye = times_right(even, tab.at[EVEN])
    yo = times_right(odd, tab.at[ODD])
    re = jnp.concatenate([ye[:, :HALF], yo[:, :HALF]], 1)
    im = jnp.concatenate([ye[:, HALF:], yo[:, HALF:]], 1)
    z_ref[0] = times_left(tab.at[EVEN_T], jnp.concatenate([re[:HALF] + re[HALF:], im[:HALF] + im[HALF:]], 0))
    z_ref[1] = times_left(tab.at[ODD_T], jnp.concatenate([re[:HALF] - re[HALF:], im[:HALF] - im[HALF:]], 0))


def inverse_transform(z_ref, out, tab):
    a = times_left(tab.at[EVEN], z_ref[0])
    b = times_left(tab.at[ODD], z_ref[1])
    total, rest = a + b, a - b
    re = jnp.concatenate([total[:HALF], rest[:HALF]], 0)
    im = jnp.concatenate([total[HALF:], rest[HALF:]], 0)
    a = times_right(jnp.concatenate([re[:, :HALF], im[:, :HALF]], 1), tab.at[EVEN_T])
    b = times_right(jnp.concatenate([re[:, HALF:], im[:, HALF:]], 1), tab.at[ODD_T])
    total, rest = a + b, a - b
    out[0] = jnp.concatenate([total[:, :HALF], rest[:, :HALF]], 1)
    out[1] = jnp.concatenate([total[:, HALF:], rest[:, HALF:]], 1)


def column_block(column, width):
    block = jnp.minimum(lax.shift_right_logical(column, 7), width // HALF - 3)
    return block, column - block * HALF


def take_window(spec, layer, component, column, width):
    block, shift = column_block(column, width)
    lane = lax.broadcasted_iota(jnp.int32, (HALF, HALF), 1)
    mixed = jnp.where(lane >= shift, spec[layer, component, block], spec[layer, component, block + 2])
    return mixed, spec[layer, component, block + 1]


def main_kernel(
    tiles, width,
    offs_hbm, spec_hbm, probe_hbm, phase_hbm, meas_hbm, tab_hbm, perm_hbm,
    grads, offs_out,
    offs, offs_table, spec, probe, phase, meas, tab, perm,
    staged, near, own_staged, own, patch, field, x_buf, z_buf, kern, update, relayed, back, offs_land,
    offs_sem, block_sem, load_sem, off_send, off_recv, in_send, in_recv, sib_send, sib_recv,
    out_send, out_recv, mid_send, mid_recv, mid_local, relay_send, relay_recv, back_send, back_recv, relay_ready,
):
    me = lax.axis_index("tile")
    core = lax.axis_index("depth")
    other = 1 - core
    has_above = me > 0
    has_below = me < tiles - 1
    above = jnp.maximum(me - 1, 0)
    below = jnp.minimum(me + 1, tiles - 1)

    row = RING * RING
    ring_rows = tiles // row
    place = lax.rem(me, row)
    far_source = (place == row - 1) & has_below & (core == 1)
    relays = (me == 0) & (core == 1)
    middle = ring_rows - 2
    passes_on = (me == middle * row - 1) & (core == 1)
    far_target = (place == 0) & has_above & (core == 1)

    barrier = pltpu.get_barrier_semaphore()
    pl.semaphore_signal(barrier, inc=1, device_id=(other, me), device_id_type=MESH)

    @pl.when(has_above)
    def _():
        for d in (0, 1):
            pl.semaphore_signal(barrier, inc=1, device_id=(d, above), device_id_type=MESH)

    row_starts = (place == 0) & has_above
    row_ends = (place == row - 1) & has_below
    early = row_starts & (core == 0)

    @pl.when(has_below)
    def _():
        pl.semaphore_signal(barrier, inc=1, device_id=(1, below), device_id_type=MESH)

    @pl.when(has_below & jnp.logical_not(row_ends))
    def _():
        pl.semaphore_signal(barrier, inc=1, device_id=(0, below), device_id_type=MESH)

    relays_back = (place == RING - 1) & (me > row) & (core == 1)
    back_source = jnp.maximum(me - 3, 0)
    back_target = jnp.maximum(me - 4, 0)

    @pl.when(relays_back)
    def _():
        pl.semaphore_signal(barrier, inc=1, device_id=(1, back_source), device_id_type=MESH)
        pl.semaphore_signal(barrier, inc=1, device_id=(1, back_target), device_id_type=MESH)

    @pl.when(relays)
    def _():
        for k in range(1, ring_rows):
            pl.semaphore_signal(barrier, inc=1, device_id=(1, k * row), device_id_type=MESH)
            if k <= middle:
                pl.semaphore_signal(barrier, inc=1, device_id=(1, k * row - 1), device_id_type=MESH)

    @pl.when(passes_on)
    def _():
        pl.semaphore_signal(barrier, inc=1, device_id=(1, (middle + 1) * row - 1), device_id_type=MESH)

    blocks = width // HALF

    def block_copy(b):
        return pltpu.make_async_copy(
            spec_hbm.at[:, :, :, pl.ds(b * HALF, HALF)], spec.at[:, :, b], block_sem.at[b]
        )

    loads = [
        pltpu.make_async_copy(tab_hbm, tab, load_sem.at[0]),
        pltpu.make_async_copy(perm_hbm, perm, load_sem.at[1]),
        pltpu.make_async_copy(probe_hbm, probe, load_sem.at[2]),
        pltpu.make_async_copy(phase_hbm, phase, load_sem.at[3]),
        pltpu.make_async_copy(meas_hbm.at[core], meas, load_sem.at[4]),
    ]
    offs_load = pltpu.make_async_copy(offs_hbm, offs, offs_sem.at[0])
    offs_store = pltpu.make_async_copy(offs_table, offs_out, offs_sem.at[1])
    offs_load.start()
    for b in range(blocks):
        block_copy(b).start()
    for copy in loads:
        copy.start()
    offs_load.wait()
    present = 1 + 2 * has_above.astype(jnp.int32) + 2 * has_below.astype(jnp.int32)
    present += 2 * (far_source | far_target).astype(jnp.int32) - 2 * early.astype(jnp.int32)
    pl.semaphore_wait(barrier, present)

    def offsets_copy(side):
        return pltpu.make_async_remote_copy(
            src_ref=offs, dst_ref=offs_land.at[1 - side], send_sem=off_send.at[side], recv_sem=off_recv.at[1 - side],
            device_id=(core, above if side == 0 else below), device_id_type=MESH,
        )

    sides = ((0, has_above), (1, has_below))
    def offsets_across():
        return pltpu.make_async_remote_copy(
            src_ref=offs, dst_ref=offs_land.at[1], send_sem=off_send.at[2], recv_sem=off_recv.at[1],
            device_id=(0, above), device_id_type=MESH,
        )

    pl.when(has_above & jnp.logical_not(early))(offsets_copy(0).start)
    pl.when(has_below)(offsets_copy(1).start)
    pl.when(row_starts & (core == 1))(offsets_across().start)

    @pl.when(far_target)
    def _():
        pl.semaphore_signal(relay_ready, inc=1, device_id=(1, 0), device_id_type=MESH)

    @pl.when(far_source)
    def _():
        pl.semaphore_signal(relay_ready, inc=1, device_id=(1, jnp.minimum(me + 4, tiles - 1)), device_id_type=MESH)

    for b in range(blocks):
        block_copy(b).wait()
    for layer in (0, 1):
        for c in (0, 1):
            mixed, pure = take_window(spec, layer, c, offs[other, 1], width)
            own_staged[layer, c, :, :HALF] = mixed
            own_staged[layer, c, :, HALF:] = pure

    def sibling_copy(layer):
        return pltpu.make_async_remote_copy(
            src_ref=own_staged.at[layer], dst_ref=own.at[2 * core + layer], send_sem=sib_send.at[layer],
            recv_sem=sib_recv.at[layer], device_id=(other, me), device_id_type=MESH,
        )

    for layer in (0, 1):
        sibling_copy(layer).start()
    for layer in (0, 1):
        for c in (0, 1):
            mixed, pure = take_window(spec, layer, c, offs[core, 1], width)
            own[2 * core + layer, c, :, :HALF] = mixed
            own[2 * core + layer, c, :, HALF:] = pure

    def window_copy(position, layer, side):
        return pltpu.make_async_remote_copy(
            src_ref=staged.at[side, position, layer], dst_ref=near.at[1 - side, 2 * core + layer],
            send_sem=in_send.at[side, position, layer], recv_sem=in_recv.at[1 - side, 2 * core + layer],
            device_id=(position, above if side == 0 else below), device_id_type=MESH,
        )

    def detour_copy(layer):
        k = me // row
        return pltpu.make_async_remote_copy(
            src_ref=staged.at[1, 1, layer], dst_ref=relayed.at[k, layer], send_sem=in_send.at[1, 1, layer],
            recv_sem=relay_recv.at[k, layer], device_id=(1, jnp.where(k == middle, middle * row - 1, 0)),
            device_id_type=MESH,
        )

    def onward_copy(layer):
        return pltpu.make_async_remote_copy(
            src_ref=relayed.at[middle, layer], dst_ref=relayed.at[middle, layer], send_sem=relay_send.at[middle, layer],
            recv_sem=relay_recv.at[middle, layer], device_id=(1, 0), device_id_type=MESH,
        )

    def relay_copy(k, layer):
        return pltpu.make_async_remote_copy(
            src_ref=relayed.at[k, layer], dst_ref=near.at[0, 2 + layer], send_sem=relay_send.at[k, layer],
            recv_sem=in_recv.at[0, 2 + layer], device_id=(1, (k + 1) * row), device_id_type=MESH,
        )

    def wait_relayed(k, layer):
        pltpu.make_async_remote_copy(
            src_ref=relayed.at[k, layer], dst_ref=relayed.at[k, layer], send_sem=relay_send.at[k, layer],
            recv_sem=relay_recv.at[k, layer], device_id=(1, row), device_id_type=MESH,
        ).wait_recv()

    def wait_offsets(side):
        pltpu.make_async_remote_copy(
            src_ref=offs, dst_ref=offs_land.at[side], send_sem=off_send.at[side], recv_sem=off_recv.at[side],
            device_id=(core, above if side == 0 else below), device_id_type=MESH,
        ).wait_recv()

    def cut(side, position, layer):
        for c in (0, 1):
            mixed, pure = take_window(spec, layer, c, offs_land[side, position, 1], width)
            staged[side, position, layer, c, :, :HALF] = mixed
            staged[side, position, layer, c, :, HALF:] = pure

    def send(side, position, layer):
        cut(side, position, layer)
        window_copy(position, layer, side).start()

    def back_direct():
        return pltpu.make_async_remote_copy(
            src_ref=staged.at[0, 1, 1, 1], dst_ref=near.at[1, 3, 1], send_sem=in_send.at[0, 1, 1],
            recv_sem=in_recv.at[1, 3], device_id=(1, above), device_id_type=MESH,
        )

    def back_detour():
        return pltpu.make_async_remote_copy(
            src_ref=staged.at[0, 1, 1, 0], dst_ref=back, send_sem=in_send.at[0, 1, 1], recv_sem=back_recv,
            device_id=(1, jnp.minimum(me + 3, tiles - 1)), device_id_type=MESH,
        )

    def back_relay():
        return pltpu.make_async_remote_copy(
            src_ref=back, dst_ref=near.at[1, 3, 0], send_sem=back_send, recv_sem=in_recv.at[1, 3],
            device_id=(1, back_target), device_id_type=MESH,
        )

    def answer(near_side):
        far_side = 1 - near_side
        for position in (0, 1):
            for side in (near_side, far_side):
                @pl.when(sides[side][1])
                def _(position=position, side=side):
                    if position == 0:
                        wait_offsets(side)
                    for layer in (0, 1):
                        if near_side == 0 and side == 1 and position == 1 and layer == 1:
                            cut(side, position, layer)
                            pl.when(far_source)(detour_copy(layer).start)
                            pl.when(jnp.logical_not(far_source))(window_copy(position, layer, side).start)
                        elif near_side == 1 and side == 0 and position == 1 and layer == 1:
                            @pl.when(jnp.logical_not(far_target))
                            def _():
                                send(0, 1, 1)
                        else:
                            send(side, position, layer)
                    if near_side == 1 and side == 0 and position == 0:
                        @pl.when(far_target)
                        def _():
                            cut(0, 1, 1)
                            back_detour().start()
                            back_direct().start()

    first_of_ring = lax.rem(me, RING) == 0
    pl.when(first_of_ring)(functools.partial(answer, 1))
    pl.when(jnp.logical_not(first_of_ring))(functools.partial(answer, 0))

    for side, there in sides:
        for position in (0, 1):
            first = offs_land[side, position, 0] - (me - 2 + 2 * side) * HALF
            offs_table[side, position, 0] = jnp.where(there, first, HALF * side)
            offs_table[side, position, 1] = jnp.where(there, offs_land[side, position, 1], 0)
    for position in (0, 1):
        offs_table[2, position, 0] = 0
        offs_table[2, position, 1] = offs[position, 1]
    offs_store.start()

    first = offs[core, 0] - (me - 1) * HALF
    unused, shift = column_block(offs[core, 1], width)
    for copy in loads:
        copy.wait()
    phases = exact_right(exact_left(perm[1], phase[...]), perm[0])
    kern[0] = jnp.cos(phases)
    kern[1] = jnp.sin(phases)
    meas[...] = exact_right(exact_left(perm[1], meas[...]), perm[0])
    rows = lax.broadcasted_iota(jnp.int32, (FULL, FULL), 0)
    cols = lax.broadcasted_iota(jnp.int32, (FULL, FULL), 1)
    turn = jnp.where(((cols + first) & (FULL - 1)) == rows, 1.0, 0.0).astype(BF16)
    slide = jnp.where(((rows + shift) & (FULL - 1)) == cols, 1.0, 0.0).astype(BF16)
    for c in (0, 1):
        field[0, c] = exact_right(exact_left(turn, probe[c]), slide)

    for layer in (0, 1):
        pltpu.make_async_remote_copy(
            src_ref=own_staged.at[layer], dst_ref=own.at[2 * other + layer], send_sem=sib_send.at[layer],
            recv_sem=sib_recv.at[layer], device_id=(other, me), device_id_type=MESH,
        ).wait_recv()

    half_rows = lax.broadcasted_iota(jnp.int32, (HALF, FULL), 0)

    def update_copy(s, side):
        target = s // 2
        return pltpu.make_async_remote_copy(
            src_ref=update.at[s, :, pl.ds(0, HALF)], dst_ref=grads.at[s - 2 * target, 2 * (1 - side) + core],
            send_sem=out_send.at[side, s], recv_sem=out_recv.at[s - 2 * target, 2 * (1 - side) + core],
            device_id=(target, above if side == 0 else below), device_id_type=MESH,
        )

    def middle_copy(layer):
        return pltpu.make_async_remote_copy(
            src_ref=update.at[2 * other + layer, :, pl.ds(HALF, HALF)], dst_ref=grads.at[layer, 4 + core],
            send_sem=mid_send.at[layer], recv_sem=mid_recv.at[layer], device_id=(other, me), device_id_type=MESH,
        )

    def middle_local(layer):
        return pltpu.make_async_copy(
            update.at[2 * core + layer, :, pl.ds(HALF, HALF)], grads.at[layer, 4 + core], mid_local.at[layer]
        )

    def step(i, carry):
        @pl.when(i <= 3)
        def _():
            for side, there in sides:
                @pl.when(there)
                def _(side=side):
                    pltpu.make_async_remote_copy(
                        src_ref=staged.at[side, 0, 0], dst_ref=near.at[side, i], send_sem=in_send.at[side, 0, 0],
                        recv_sem=in_recv.at[side, i], device_id=(core, above if side == 0 else below),
                        device_id_type=MESH,
                    ).wait_recv()
            top = [jnp.where(half_rows >= first, near[0, i, c], near[1, i, c]) for c in (0, 1)]
            bottom = [own[i, c] for c in (0, 1)]
            for c in (0, 1):
                patch[i, c, :HALF] = top[c]
                patch[i, c, HALF:] = bottom[c]
            for part, (pr, pi) in enumerate((top, bottom)):
                span = pl.ds(part * HALF, HALF)
                wr, wi = field[i, 0, span], field[i, 1, span]
                x_buf[0, span] = wr * pr - wi * pi
                x_buf[1, span] = wr * pi + wi * pr

        @pl.when(i > 3)
        def _():
            pr, pi = patch[7 - i, 0], patch[7 - i, 1]
            ar, ai = field[i, 0], field[i, 1]
            x_buf[0] = pr * ar + pi * ai
            x_buf[1] = pr * ai - pi * ar

        @pl.when(passes_on & (i == 0))
        def _():
            for layer in DETOURED:
                wait_relayed(middle, layer)
                onward_copy(layer).start()

        @pl.when(relays_back & (i == 1))
        def _():
            pl.semaphore_wait(relay_ready, 1)
            pltpu.make_async_remote_copy(
                src_ref=back, dst_ref=back, send_sem=back_send, recv_sem=back_recv,
                device_id=(1, back_source), device_id_type=MESH,
            ).wait_recv()
            back_relay().start()

        @pl.when(relays & (i == 1))
        def _():
            pl.semaphore_wait(relay_ready, ring_rows - 1)
            for k in range(ring_rows - 1):
                for layer in DETOURED:
                    wait_relayed(k, layer)
                    relay_copy(k, layer).start()

        forward_transform(x_buf, z_buf, tab)

        @pl.when(i == 3)
        def _():
            for parity in (0, 1):
                zr, zi = z_buf[parity, :HALF], z_buf[parity, HALF:]
                e = 2.0 * (zr * zr + zi * zi - meas[parity * HALF : (parity + 1) * HALF])
                z_buf[parity, :HALF] = e * zr
                z_buf[parity, HALF:] = e * zi

        @pl.when(i != 3)
        def _():
            sign = jnp.where(i < 3, 1.0, -1.0)
            for parity in (0, 1):
                span = slice(parity * HALF, (parity + 1) * HALF)
                zr, zi = z_buf[parity, :HALF], z_buf[parity, HALF:]
                kr, ki = kern[0, span], sign * kern[1, span]
                z_buf[parity, :HALF] = kr * zr - ki * zi
                z_buf[parity, HALF:] = kr * zi + ki * zr

        inverse_transform(z_buf, field.at[i + 1], tab)

        @pl.when(i >= 3)
        def _():
            s = 6 - i
            wr, wi = field[s, 0], field[s, 1]
            ar, ai = field[i + 1, 0], field[i + 1, 1]
            update[s, 0] = wr * ar + wi * ai
            update[s, 1] = wr * ai - wi * ar
            for side, there in sides:
                @pl.when(there)
                def _(side=side):
                    update_copy(s, side).start()
            for layer in (0, 1):
                pl.when(s == 2 * other + layer)(middle_copy(layer).start)
                pl.when(s == 2 * core + layer)(middle_local(layer).start)

        return carry

    lax.fori_loop(0, 7, step, 0)

    offs_store.wait()
    for k in range(ring_rows - 1):
        for layer in DETOURED:
            pl.when(relays)(relay_copy(k, layer).wait_send)
    for layer in DETOURED:
        pl.when(passes_on)(onward_copy(layer).wait_send)
    pl.when(has_above & jnp.logical_not(early))(offsets_copy(0).wait_send)
    pl.when(has_below)(offsets_copy(1).wait_send)
    pl.when(row_starts & (core == 1))(offsets_across().wait_send)
    pl.when(relays_back)(back_relay().wait_send)
    for layer in (0, 1):
        middle_local(layer).wait()
        middle_copy(layer).wait_send()
        pltpu.make_async_remote_copy(
            src_ref=update.at[0, :, pl.ds(HALF, HALF)], dst_ref=grads.at[layer, 4 + other],
            send_sem=mid_send.at[layer], recv_sem=mid_recv.at[layer], device_id=(other, me), device_id_type=MESH,
        ).wait_recv()
        sibling_copy(layer).wait_send()
    for side, there in sides:
        @pl.when(there)
        def _(side=side):
            for position in (0, 1):
                for layer in (0, 1):
                    window_copy(position, layer, side).wait_send()
            for s in range(4):
                update_copy(s, side).wait_send()
            for layer in (0, 1):
                for position in (0, 1):
                    pltpu.make_async_remote_copy(
                        src_ref=update.at[0, :, pl.ds(0, HALF)], dst_ref=grads.at[layer, 2 * side + position],
                        send_sem=out_send.at[side, 0], recv_sem=out_recv.at[layer, 2 * side + position],
                        device_id=(core, above if side == 0 else below), device_id_type=MESH,
                    ).wait_recv()


def place_kernel(width, offs_hbm, grads, out, offs, held, strip, offs_sem, in_sem, out_sem):
    def in_copy(layer, c):
        return pltpu.make_async_copy(grads.at[layer, :, c], held.at[layer, c], in_sem.at[layer, c])

    def out_copy(layer, c):
        return pltpu.make_async_copy(strip.at[layer, c], out.at[layer, c], out_sem.at[layer, c])

    parts = [(layer, c) for layer in (0, 1) for c in (0, 1)]
    offs_load = pltpu.make_async_copy(offs_hbm, offs, offs_sem)
    offs_load.start()
    for part in parts:
        in_copy(*part).start()
    strip[...] = jnp.zeros_like(strip)
    row = lax.broadcasted_iota(jnp.int32, (HALF, FULL), 0)
    lane = lax.broadcasted_iota(jnp.int32, (HALF, HALF), 1)
    offs_load.wait()
    for layer, c in parts:
        in_copy(layer, c).wait()
        for window in range(6):
            side, position = window // 2, window % 2
            block, shift = column_block(offs[side, position, 1], width)
            value = held[layer, c, window]
            if side == 0:
                value = jnp.where(row < offs[0, position, 0], value, 0.0)
            elif side == 1:
                value = jnp.where(row >= offs[1, position, 0], value, 0.0)
            mixed, pure = value[:, :HALF], value[:, HALF:]
            first = lane >= shift
            for k, piece in enumerate((jnp.where(first, mixed, 0.0), pure, jnp.where(first, 0.0, mixed))):
                span = pl.ds(pl.multiple_of((block + k) * HALF, HALF), HALF)
                strip[layer, c, :, span] += piece
        out_copy(layer, c).start()
    for part in parts:
        out_copy(*part).wait()


def local(tiles, specimen, scan_offsets, probe_wave, fresnel_phase, measured):
    width = specimen.shape[3]
    any_space = pl.BlockSpec(memory_space=pl.ANY)
    dma = pltpu.SemaphoreType.DMA
    vm = lambda *shape: pltpu.VMEM(shape, F32)
    grads, near_offs = pl.pallas_call(
        functools.partial(main_kernel, tiles, width),
        out_shape=[
            jax.ShapeDtypeStruct((2, 6, 2, HALF, FULL), F32),
            jax.ShapeDtypeStruct((3, 2, 2), jnp.int32),
        ],
        in_specs=[any_space] * 7,
        out_specs=[any_space, any_space],
        scratch_shapes=[
            pltpu.SMEM((2, 2), jnp.int32),
            pltpu.SMEM((3, 2, 2), jnp.int32),
            vm(2, 2, width // HALF, HALF, HALF),
            vm(2, FULL, FULL),
            vm(FULL, FULL),
            vm(FULL, FULL),
            pltpu.VMEM((4, 2, FULL, FULL), BF16),
            pltpu.VMEM((2, FULL, FULL), BF16),
            vm(2, 2, 2, 2, HALF, FULL),
            vm(2, 4, 2, HALF, FULL),
            vm(2, 2, HALF, FULL),
            vm(4, 2, HALF, FULL),
            vm(4, 2, FULL, FULL),
            vm(8, 2, FULL, FULL),
            vm(2, FULL, FULL),
            vm(2, FULL, FULL),
            vm(2, FULL, FULL),
            vm(4, 2, FULL, FULL),
            vm(tiles // (RING * RING) - 1, 2, 2, HALF, FULL),
            vm(HALF, FULL),
            pltpu.SMEM((2, 2, 2), jnp.int32),
            dma((2,)), dma((width // HALF,)), dma((5,)),
            dma((3,)), dma((2,)),
            dma((2, 2, 2)), dma((2, 4)),
            dma((2,)), dma((2,)),
            dma((2, 4)), dma((2, 4)),
            dma((2,)), dma((2,)), dma((2,)),
            dma((tiles // (RING * RING) - 1, 2)), dma((tiles // (RING * RING) - 1, 2)),
            dma, dma, pltpu.SemaphoreType.REGULAR,
        ],
        compiler_params=pltpu.CompilerParams(
            collective_id=0, has_side_effects=True, vmem_limit_bytes=60 * 2**20
        ),
        name="ptycho",
    )(scan_offsets, specimen, probe_wave, fresnel_phase, measured, jnp.asarray(dft_tables()), jnp.asarray(order_tables()))
    return pl.pallas_call(
        functools.partial(place_kernel, width),
        out_shape=jax.ShapeDtypeStruct(specimen.shape, F32),
        in_specs=[any_space, any_space],
        out_specs=any_space,
        scratch_shapes=[
            pltpu.SMEM((3, 2, 2), jnp.int32), vm(2, 2, 6, HALF, FULL), vm(2, 2, HALF, width),
            dma, dma((2, 2)), dma((2, 2)),
        ],
        compiler_params=pltpu.CompilerParams(vmem_limit_bytes=60 * 2**20),
        name="place",
    )(near_offs, grads)


def solution(mesh):
    placed = (P("depth", None, "tile", None), P("tile", None), P(), P(), P("tile", None, None))
    return jax.shard_map(
        functools.partial(local, mesh.shape["tile"]),
        mesh=mesh, in_specs=placed, out_specs=P("depth", None, "tile", None), check_vma=False,
    )
```
